128 devices in a mesh: section: 2 (over core), dp: 16 (over z, y), tensor: 4 (over x).
Axes of the slice: x: 4, y: 4, z: 4, core: 2. Of those that a mesh axis runs over, the one named last changes fastest.
Arguments:
- inputs: bfloat16 [2, 4096, 1024], P(None, ('dp', 'tensor')), may hold values from -6 to 6
- cotangent: bfloat16 [2, 4096, 1024], P(None, ('dp', 'tensor')), may hold values from -6 to 6
- w_qkv: bfloat16 [2, 1024, 3, 1024], P('section', 'dp', None, 'tensor'), may hold values from -0.25 to 0.25
- b_qkv: float32 [2, 3, 1024], P('section', None, 'tensor'), may hold values from -2 to 2
- w_out: bfloat16 [2, 1024, 1024], P('section', 'tensor', 'dp'), may hold values from -0.5 to 0.5
- w_fc: bfloat16 [2, 1024, 4096], P('section', 'dp', 'tensor'), may hold values from -0.1875 to 0.1875
- b_fc: float32 [2, 4096], P('section', 'tensor'), may hold values from -3 to 3
- w_proj: bfloat16 [2, 4096, 1024], P('section', 'tensor', 'dp'), may hold values from -0.09375 to 0.09375
- norm_gains: float32 [2, 2, 1024], P('section'), may hold values from 0.1 to 1.9
- norm_shifts: float32 [2, 4, 1024], P('section'), may hold values from -2 to 2
- seq_lengths: int32 [64], replicated, may hold values from 1 to 256, as said below
- seq_ranks: int32 [64], replicated, may hold values from 0 to 15
- seq_micros: int32 [64], replicated, may hold values from 0 to 1
Outputs:
- activations: bfloat16 [2, 2, 4096, 1024], P('section', None, ('dp', 'tensor'))
- input_grads: bfloat16 [2, 2, 4096, 1024], P('section', None, ('dp', 'tensor'))
- grad_w_qkv: float32 [2, 1024, 3, 1024], P('section', 'dp', None, 'tensor')
- grad_b_qkv: float32 [2, 3, 1024], P('section', None, 'tensor')
- grad_w_out: float32 [2, 1024, 1024], P('section', 'tensor', 'dp')
- grad_w_fc: float32 [2, 1024, 4096], P('section', 'dp', 'tensor')
- grad_b_fc: float32 [2, 4096], P('section', 'tensor')
- grad_w_proj: float32 [2, 4096, 1024], P('section', 'tensor', 'dp')
- grad_norm_gains: float32 [2, 2, 1024], P('section')
- grad_norm_shifts: float32 [2, 4, 1024], P('section')
The draws below stay inside these ranges and needn't reach their ends.
Inputs may be any that keep to these rules, and one draw needn't show every extreme that they name: `seq_lengths`: the sequences of one slot (data rank and micro-batch) hold at most 256 tokens together and fill its rows in order of their index; every slot holds one or more sequences; in every draw one sequence, alone in its slot, has exactly 256 tokens.
All inputs are finite; a program needn't handle non-finite values.
Results may differ from the reference program's by a relative error of at most 0.035.
Values may be sent and summed in bfloat16 or wider, within the bound.
A program may use at most 128 MiB of HBM per device.

```python
import jax
import jax.numpy as jnp
from jax import lax

D = 1024
H = 16
HD = 64
FF = 4096
ROWS = 256
MB = 2
TOKENS = 4096
SEQS = 64
N_DP = 16


def seq_layout(key):
    slot_count = N_DP * MB
    keys = jax.random.split(key, 5)
    first = jax.random.permutation(keys[0], slot_count).astype(jnp.int32)
    full = jax.random.randint(keys[1], (), 0, slot_count, dtype=jnp.int32)
    extra = (full + 1 + jax.random.randint(keys[2], (SEQS - slot_count,), 0, slot_count - 1, dtype=jnp.int32)) % slot_count
    owner = jnp.concatenate([first, extra]).astype(jnp.int32)
    slot_ids = jnp.arange(slot_count, dtype=jnp.int32)
    onehot = (owner[:, None] == slot_ids[None, :]).astype(jnp.int32)
    counts = jnp.sum(onehot, axis=0, dtype=jnp.int32)
    divisor = 1 + jax.random.randint(keys[3], (slot_count,), 0, 3, dtype=jnp.int32)
    fills = jnp.maximum(ROWS // divisor, counts)
    fills = jnp.where(slot_ids == full, ROWS, fills).astype(jnp.int32)
    shares = jax.random.randint(keys[4], (SEQS,), 1, 8, dtype=jnp.int32)
    totals = jnp.sum(onehot * shares[:, None], axis=0, dtype=jnp.int32)
    room = jnp.sum(onehot * (fills - counts)[None, :], axis=1, dtype=jnp.int32)
    whole = jnp.sum(onehot * totals[None, :], axis=1, dtype=jnp.int32)
    lengths = 1 + room * shares // whole
    return (lengths.astype(jnp.int32), (owner // MB).astype(jnp.int32), (owner % MB).astype(jnp.int32))


def draw_seq_lengths(key, part):
    shared = seq_layout(key)
    return shared[0]


def draw_seq_ranks(key, part):
    shared = seq_layout(key)
    return shared[1]


def draw_seq_micros(key, part):
    shared = seq_layout(key)
    return shared[2]


def level_of(stream_key, shape, cuts, low, high):
    def one(axis_at, blocks):
        draws = jax.random.uniform(jax.random.fold_in(jax.random.fold_in(stream_key, 6), axis_at), (blocks,), jnp.float32, low / len(cuts), high / len(cuts))
        return jnp.repeat(jnp.exp(draws), shape[axis_at] // blocks).reshape((-1,) + (1,) * (len(shape) - axis_at - 1))

    factor_of = one(*cuts[0])
    for cut in cuts[1:]:
        factor_of = factor_of * one(*cut)
    return factor_of


def centred(stream_key, shape, scale, bound, cuts=(), held_as=jnp.bfloat16):
    array = scale * jax.random.normal(stream_key, shape, jnp.float32)
    if cuts:
        array = array * level_of(stream_key, shape, cuts, -0.22, 0.18)
    return jnp.clip(array, -bound, bound).astype(held_as)


def setup_inputs(seed: int = 0) -> dict:
    key_list = jax.random.split(jax.random.key(seed), 14)
    return {
        "inputs": centred(key_list[0], (MB, TOKENS, D), 1.0, 6.0, ((1, 64),)),
        "cotangent": centred(key_list[1], (MB, TOKENS, D), 1.0, 6.0, ((1, 64),)),
        "w_qkv": centred(key_list[2], (2, D, 3, D), (D // 2) ** -0.5, 0.25, ((0, 2), (1, 16), (3, 4))),
        "b_qkv": centred(key_list[3], (2, 3, D), 0.3, 2.0, ((0, 2), (2, 4)), jnp.float32),
        "w_out": centred(key_list[4], (2, D, D), (D // 8) ** -0.5, 0.5, ((0, 2), (1, 4), (2, 16))),
        "w_fc": centred(key_list[5], (2, D, FF), D ** -0.5, 0.1875, ((0, 2), (1, 16), (2, 4))),
        "b_fc": centred(key_list[6], (2, FF), 0.5, 3.0, ((0, 2), (1, 4)), jnp.float32),
        "w_proj": centred(key_list[7], (2, FF, D), FF ** -0.5, 0.09375, ((0, 2), (1, 4), (2, 16))),
        "norm_gains": jnp.clip(1.0 + 0.18 * jax.random.normal(key_list[8], (2, 2, D), jnp.float32), 0.1, 1.9),
        "norm_shifts": centred(key_list[9], (2, 4, D), 0.3, 2.0, ((0, 2),), jnp.float32),
        "seq_lengths": draw_seq_lengths(jax.random.fold_in(key_list[13], 71), 0),
        "seq_ranks": draw_seq_ranks(jax.random.fold_in(key_list[13], 71), 0),
        "seq_micros": draw_seq_micros(jax.random.fold_in(key_list[13], 71), 0),
    }


@jax.custom_vjp
def low(v):
    return lax.optimization_barrier(v.astype(jnp.bfloat16)).astype(jnp.float32)

@jax.custom_vjp
def low_back(v):
    return v

def low_keep(v):
    return (low(v), None)

def low_pass(kept, grad):
    return (grad,)

def back_keep(v):
    return (v, None)

def back_low(kept, grad):
    return (low(grad),)
low.defvjp(low_keep, low_pass)
low_back.defvjp(back_keep, back_low)
HIGHEST = lax.Precision.HIGHEST
epsilon = 1e-05

def slot_labels(lengths, ranks, micros, rank_now, micro_now, row_count):
    mine = (ranks == rank_now) & (micros == micro_now)
    taken = jnp.where(mine, lengths, 0).astype(jnp.int32)
    ends = jnp.cumsum(taken, dtype=jnp.int32)
    starts = ends - taken
    places = jnp.arange(row_count, dtype=jnp.int32)[:, None]
    inside = mine[None, :] & (places >= starts[None, :]) & (places < ends[None, :])
    numbers = jnp.arange(lengths.shape[0], dtype=jnp.int32)[None, :] + 1
    return lax.optimization_barrier(jnp.sum(jnp.where(inside, numbers, 0), axis=1, dtype=jnp.int32)) - 1

def allowed(label_rows, label_cols, place_rows, place_cols):
    same = (label_rows[:, None] == label_cols[None, :]) & (label_rows[:, None] >= 0)
    causal = place_cols[None, :] <= place_rows[:, None]
    return same & causal | (place_rows[:, None] == place_cols[None, :])

def layer_norm(values, gain_row, shift_row):
    average = lax.optimization_barrier(jnp.mean(values, axis=-1, keepdims=True))
    centered = values - average
    variance = lax.optimization_barrier(jnp.mean(centered * centered, axis=-1, keepdims=True))
    return centered * lax.rsqrt(variance + epsilon) * gain_row + shift_row

def attention(queries, key_heads, value_heads, labels):
    row_count = queries.shape[0]
    block_rows = min(512, row_count)
    block_count = row_count // block_rows
    places = jnp.arange(row_count, dtype=jnp.int32)
    factor = HD ** (-0.5)

    def one_block(pieces):
        query_block, label_block, place_block = pieces
        scores = jnp.einsum('qhe,khe->hqk', query_block, key_heads, precision=HIGHEST) * factor
        scores = low_back(scores)
        visible = allowed(label_block, labels, place_block, places)
        scores = jnp.where(visible[None], scores, -1e+30)
        weights_low = low(jax.nn.softmax(scores, axis=-1))
        return jnp.einsum('hqk,khe->qhe', weights_low, value_heads, precision=HIGHEST)
    shaped = (queries.reshape(block_count, block_rows, H, HD), labels.reshape(block_count, block_rows), places.reshape(block_count, block_rows))
    outputs = lax.map(jax.checkpoint(one_block), shaped)
    return outputs.reshape(row_count, H * HD)

def layer_apply(params, values, labels):
    w_qkv, b_qkv, w_out, w_fc, b_fc, w_proj, gains, shifts = params
    row_count = values.shape[0]
    normed_first = low(layer_norm(values, gains[0], shifts[0]))
    projected = jnp.einsum('rd,dcf->rcf', normed_first, w_qkv, precision=HIGHEST) + b_qkv[None]
    projected = low_back(low(projected))
    queries = projected[:, 0].reshape(row_count, H, HD)
    key_heads = projected[:, 1].reshape(row_count, H, HD)
    value_heads = projected[:, 2].reshape(row_count, H, HD)
    attended = low_back(low(attention(queries, key_heads, value_heads, labels)))
    branch = low_back(jnp.dot(attended, w_out, precision=HIGHEST, preferred_element_type=jnp.float32))
    hidden = values + branch + shifts[2]
    normed_second = low(layer_norm(hidden, gains[1], shifts[1]))
    gelu_input = low_back(jnp.dot(normed_second, w_fc, precision=HIGHEST, preferred_element_type=jnp.float32) + b_fc)
    activated = low(jax.nn.gelu(gelu_input, approximate=True))
    branch_second = low_back(jnp.dot(activated, w_proj, precision=HIGHEST, preferred_element_type=jnp.float32))
    output = hidden + branch_second + shifts[3]
    return output * (labels >= 0).astype(jnp.float32)[:, None]

def arrange(stacked):
    shaped = stacked.reshape(N_DP, MB, ROWS, D)
    return jnp.transpose(shaped, (1, 0, 2, 3)).reshape(MB, N_DP * ROWS, D)

def reference(inputs, cotangent, w_qkv, b_qkv, w_out, w_fc, b_fc, w_proj, norm_gains, norm_shifts, seq_lengths, seq_ranks, seq_micros):
    stacked = [w_qkv, b_qkv, w_out, w_fc, b_fc, w_proj, norm_gains, norm_shifts]
    params_first = tuple((item[0].astype(jnp.float32) for item in stacked))
    params_second = tuple((item[1].astype(jnp.float32) for item in stacked))
    zero_totals = jax.tree.map(jnp.zeros_like, (params_first, params_second))

    def per_slot(totals, slot_index):
        rank_now = (slot_index // MB).astype(jnp.int32)
        micro_now = (slot_index % MB).astype(jnp.int32)
        labels = slot_labels(seq_lengths, seq_ranks, seq_micros, rank_now, micro_now, ROWS)
        start_row = (rank_now * ROWS).astype(jnp.int32)
        anchor = jnp.zeros((), jnp.int32)
        slot_in = lax.dynamic_slice(inputs, (micro_now, start_row, anchor), (1, ROWS, D))[0].astype(jnp.float32)
        slot_cot = lax.dynamic_slice(cotangent, (micro_now, start_row, anchor), (1, ROWS, D))[0].astype(jnp.float32)

        def sections(first_params, second_params, first_in, extra):
            first_out = layer_apply(first_params, first_in, labels)
            sent = low_back(low(first_out))
            second_out = layer_apply(second_params, sent + extra, labels)
            return (first_out, second_out)
        outs_pair, pullback = jax.vjp(sections, params_first, params_second, slot_in, jnp.zeros_like(slot_in))
        grads = pullback((jnp.zeros_like(slot_in), slot_cot))
        totals = jax.tree.map(jnp.add, totals, (grads[0], grads[1]))
        return (totals, (outs_pair[0], outs_pair[1], grads[2], grads[3]))
    totals, results = lax.scan(per_slot, zero_totals, jnp.arange(N_DP * MB, dtype=jnp.int32))
    activations = jnp.stack([arrange(results[0]), arrange(results[1])]).astype(jnp.bfloat16)
    input_grads = jnp.stack([arrange(results[2]), arrange(results[3])]).astype(jnp.bfloat16)
    grads_first, grads_second = totals
    merged = [jnp.stack([grads_first[index], grads_second[index]]) for index in range(8)]
    return (activations, input_grads, merged[0], merged[1], merged[2], merged[3], merged[4], merged[5], merged[6], merged[7])
```

```python
import jax
import jax.numpy as jnp
from jax import lax
from jax.experimental import pallas as pl
from jax.experimental.pallas import tpu as pltpu
from jax.sharding import PartitionSpec as P

HD = 64
EPS = 1e-05
MESH = pl.DeviceIdType.MESH
F32 = jnp.float32
BF16 = jnp.bfloat16
GELU_A = 0.7978845608028654
GELU_B = 0.044715


def nn(a, b):
    return lax.dot_general(a, b, (((1,), (0,)), ((), ())), preferred_element_type=F32)


def nt(a, b):
    return lax.dot_general(a, b, (((1,), (1,)), ((), ())), preferred_element_type=F32)


def tn(a, b):
    return lax.dot_general(a, b, (((0,), (0,)), ((), ())), preferred_element_type=F32)


def norm(values):
    average = jnp.mean(values, axis=-1, keepdims=True)
    centered = values - average
    inv = lax.rsqrt(jnp.mean(centered * centered, axis=-1, keepdims=True) + EPS)
    return centered * inv, inv


def norm_back(grad, normal, inv, gain):
    scaled = grad * gain
    return inv * (
        scaled
        - jnp.mean(scaled, axis=-1, keepdims=True)
        - normal * jnp.mean(scaled * normal, axis=-1, keepdims=True)
    )


def gelu(u):
    return 0.5 * u * (1.0 + jnp.tanh(GELU_A * (u + GELU_B * u * u * u)))


def gelu_slope(u):
    square = u * u
    t = jnp.tanh(GELU_A * u * (1.0 + GELU_B * square))
    return 0.5 * (1.0 + t) + 0.5 * u * (1.0 - t * t) * (GELU_A * (1.0 + 3.0 * GELU_B * square))


class Sizes:
    def __init__(self, z, y, t, rows, width, heads, hidden):
        self.Z, self.Y, self.T = z, y, t
        self.LR, self.D, self.E, self.F = rows, width, heads, hidden
        self.R = rows * t
        self.C = 2
        self.DC = width // self.C
        self.B = width // (z * y)
        self.HB = self.B // 2
        self.names = ("q", "o", "f", "p")
        self.width = {"q": 3 * heads, "o": heads, "f": hidden, "p": hidden}


def kernel_body(sz, n_sems, *refs):
    names = sz.names
    Z, Y, T, LR, D, E, F, R = sz.Z, sz.Y, sz.T, sz.LR, sz.D, sz.E, sz.F, sz.R
    C, DC, HB, B = sz.C, sz.DC, sz.HB, sz.B
    it = iter(refs)
    x_in, cot_in = next(it), next(it)
    shard = {m: next(it) for m in names}
    pack_in, seq_in = next(it), next(it)
    act_out, grad_out = next(it), next(it)
    gout = {m: next(it) for m in names}
    small_out = next(it)
    W = {m: next(it) for m in names}
    G = {m: next(it) for m in names}
    SIB = {m: next(it) for m in names}
    RA = {m: next(it) for m in names}
    RB = {m: next(it) for m in names}
    R2A = {m: next(it) for m in names}
    R2B = {m: next(it) for m in names}
    pack = next(it)
    A, Cn, DM, DH = next(it), next(it), next(it), next(it)
    QKV, O, PR, U, Gl = next(it), next(it), next(it), next(it), next(it)
    DU, DO, DQKV = next(it), next(it), next(it)
    N1, I1, N2, I2 = next(it), next(it), next(it), next(it)
    HID = next(it)
    MASK = next(it)
    stage, recv = next(it), next(it)
    small, small_sib, small_x, small_y, small_z = next(it), next(it), next(it), next(it), next(it)
    act_send, act_recv, ig_send, ig_recv = next(it), next(it), next(it), next(it)
    send_sem, recv_sem = next(it), next(it)

    s = lax.axis_index("section")
    d = lax.axis_index("dp")
    t = lax.axis_index("tensor")
    z = d // Y
    y = d % Y
    count = [0]
    drains = []

    def copy(src, dst, device, when=None):
        i = count[0]
        count[0] += 1
        c = pltpu.make_async_remote_copy(
            src_ref=src,
            dst_ref=dst,
            send_sem=send_sem.at[i],
            recv_sem=recv_sem.at[i],
            device_id=device,
            device_id_type=MESH,
        )
        drains.append((c, when))
        return c

    def at_x(k):
        return (s, d, (t + k) % T)

    def at_y(k):
        return (s, z * Y + (y + k) % Y, t)

    def at_z(k):
        return (s, ((z + k) % Z) * Y + y, t)

    sibling = (1 - s, d, t)

    def far_first(n):
        return sorted(range(1, n), key=lambda k: -min(k, n - k))

    barrier = pltpu.get_barrier_semaphore()
    peers = (
        [at_x(k) for k in range(1, T)]
        + [at_y(k) for k in range(1, Y)]
        + [at_z(k) for k in range(1, Z)]
        + [sibling]
    )
    for p in peers:
        pl.semaphore_signal(barrier, inc=1, device_id=p, device_id_type=MESH)

    for m in names:
        W[m][s, z, y] = shard[m][...]
    pack[s] = pack_in[...]
    pl.semaphore_wait(barrier, len(peers))

    pack_copy = copy(pack.at[s], pack.at[s], sibling)
    pack_copy.start()

    class Gather:
        def __init__(self, l, m):
            w = W[m]
            self.one_a = [
                copy(w.at[l, z, y, pl.ds(0, HB)], w.at[l, z, y, pl.ds(0, HB)], at_y(k), l)
                for k in far_first(Y)
            ]
            self.one_b = [
                copy(w.at[l, z, y, pl.ds(HB, HB)], w.at[l, z, y, pl.ds(HB, HB)], at_z(k), l)
                for k in far_first(Z)
            ]
            self.two_a = [
                copy(w.at[l, z, :, pl.ds(0, HB)], w.at[l, z, :, pl.ds(0, HB)], at_z(k), l)
                for k in far_first(Z)
            ]
            self.two_b = [
                copy(w.at[l, :, y, pl.ds(HB, HB)], w.at[l, :, y, pl.ds(HB, HB)], at_y(k), l)
                for k in far_first(Y)
            ]
            self.over = copy(w.at[l], w.at[l], sibling, l)

        def one(self):
            for c in self.one_a + self.one_b:
                c.start()

        def two(self):
            for c in self.one_a:
                c.wait_recv()
            for c in self.two_a:
                c.start()
            for c in self.one_b:
                c.wait_recv()
            for c in self.two_b:
                c.start()

        def three(self):
            for c in self.two_a + self.two_b:
                c.wait_recv()
            self.over.start()

        def arrive(self):
            self.over.wait_recv()

    gathers = [{m: Gather(l, m) for m in names} for l in range(2)]

    def on(core, f):
        pl.when(s == core)(f)

    def phase(l, step, *ms):
        def go():
            for m in ms:
                getattr(gathers[l][m], step)()

        on(l, go)

    def ready(l, m):
        on(l, gathers[l][m].three)
        on(1 - l, gathers[l][m].arrive)

    phase(0, "one", "q", "o", "f", "p")

    seqs = seq_in[...].astype(F32)
    n_seq = seqs.shape[1]
    lengths, ranks, micros = seqs[0:1], seqs[1:2], seqs[2:3]
    mine_row = jnp.logical_and(ranks == d.astype(F32), micros == s.astype(F32))
    taken_row = jnp.where(mine_row, lengths, 0.0)
    i0 = lax.broadcasted_iota(jnp.int32, (n_seq, n_seq), 0)
    i1 = lax.broadcasted_iota(jnp.int32, (n_seq, n_seq), 1)
    taken_col = jnp.sum(jnp.where(i0 == i1, taken_row, 0.0), axis=1, keepdims=True)
    ends_col = jnp.sum(jnp.where(i1 <= i0, taken_row, 0.0), axis=1, keepdims=True)
    ends_row = jnp.sum(jnp.where(i0 <= i1, taken_col, 0.0), axis=0, keepdims=True)
    number_row = lax.broadcasted_iota(jnp.int32, (1, n_seq), 1).astype(F32) + 1.0
    number_col = lax.broadcasted_iota(jnp.int32, (n_seq, 1), 0).astype(F32) + 1.0

    def column_labels(rows, first):
        places = (lax.broadcasted_iota(jnp.int32, (rows, n_seq), 0) + first).astype(F32)
        inside = jnp.logical_and(places >= ends_row - taken_row, places < ends_row)
        return jnp.sum(jnp.where(inside, number_row, 0.0), axis=1, keepdims=True)

    label_col = column_labels(R, 0)
    places = lax.broadcasted_iota(jnp.int32, (n_seq, R), 1).astype(F32)
    inside = jnp.logical_and(places >= ends_col - taken_col, places < ends_col)
    label_row = jnp.sum(jnp.where(inside, number_col, 0.0), axis=0, keepdims=True)
    r0 = lax.broadcasted_iota(jnp.int32, (R, R), 0)
    r1 = lax.broadcasted_iota(jnp.int32, (R, R), 1)
    same = jnp.logical_and(label_col == label_row, label_col > 0.5)
    visible = jnp.logical_or(jnp.logical_and(same, r1 <= r0), r0 == r1)
    MASK[...] = jnp.where(visible, 1.0, 0.0)
    valid = jnp.where(column_labels(LR, t * LR) > 0.5, 1.0, 0.0)

    pack_copy.wait_recv()

    def gain(l, i):
        return pack[l, i : i + 1, :]

    def shift(l, i):
        return pack[l, 2 + i : 3 + i, :]

    def gather_x(buf):
        copies = [copy(buf.at[t], buf.at[t], at_x(k)) for k in far_first(T)]
        for c in copies:
            c.start()

        def wait():
            for c in copies:
                c.wait_recv()

        return wait

    stage_busy = {}
    stage_turn = [0]

    def scatter_x(part):
        turn = stage_turn[0]
        stage_turn[0] += 1
        slot = turn % 2
        for c in stage_busy.get(slot, []):
            c.wait_send()
            drains[:] = [p for p in drains if p[0] is not c]
        copies = []
        for c in range(C):
            stage[slot, c] = part(c).astype(BF16).reshape(T, LR, DC)
            for k in far_first(T):
                one = copy(stage.at[slot, c, (t + k) % T], recv.at[turn, c, k - 1], at_x(k))
                one.start()
                copies.append(one)
        stage_busy[slot] = copies

        def total():
            for c in copies:
                c.wait_recv()
            out = []
            for c in range(C):
                v = stage[slot, c, t].astype(F32)
                for k in range(1, T):
                    v = v + recv[turn, c, k - 1].astype(F32)
                out.append(v)
            return jnp.concatenate(out, axis=1)

        return total

    lanes = lax.broadcasted_iota(jnp.int32, (R, 2 * HD), 1)

    def half(v, h):
        keep = lanes < HD if h == 0 else lanes >= HD
        return jnp.where(keep, v, jnp.zeros_like(v))

    factor = HD ** (-0.5)

    def rows_of(buf):
        return buf[...].reshape(R, D)

    def weight(m, l):
        return W[m][l].reshape(D, sz.width[m])

    def weight_rows(m, l, c):
        span = Z // C
        return W[m][l, c * span : (c + 1) * span].reshape(DC, sz.width[m])

    def layer_forward(l, X, at_a, at_b, at_c, at_d):
        n1, inv1 = norm(X)
        N1[l] = n1
        I1[l] = inv1
        A[l, t] = (n1 * gain(l, 0) + shift(l, 0)).astype(BF16)
        wait = gather_x(A.at[l])
        at_a()
        ready(l, "q")
        wait()
        bias = pack[l, 7:8, : 3 * E]
        QKV[l] = (nn(rows_of(A.at[l]), weight("q", l)) + bias).astype(BF16)
        for pair in range(E // (2 * HD)):
            lo = pair * 2 * HD
            q2 = QKV[l, :, lo : lo + 2 * HD]
            k2 = QKV[l, :, E + lo : E + lo + 2 * HD]
            v2 = QKV[l, :, 2 * E + lo : 2 * E + lo + 2 * HD]
            o2 = None
            for h in range(2):
                S = nt(q2, half(k2, h)) * factor
                S = jnp.where(MASK[...] > 0.5, S, -1e30)
                e = jnp.exp(S - jnp.max(S, axis=-1, keepdims=True))
                pr = (e / jnp.sum(e, axis=-1, keepdims=True)).astype(BF16)
                PR[l, pair * 2 + h] = pr
                part = nn(pr, half(v2, h))
                o2 = part if o2 is None else o2 + part
            O[l, :, lo : lo + 2 * HD] = o2.astype(BF16)
        ready(l, "o")
        total = scatter_x(lambda c: nt(O[l], weight_rows("o", l, c)))
        at_b()
        hidden = X + total() + shift(l, 2)
        n2, inv2 = norm(hidden)
        N2[l] = n2
        I2[l] = inv2
        HID[...] = hidden
        Cn[l, t] = (n2 * gain(l, 1) + shift(l, 1)).astype(BF16)
        wait = gather_x(Cn.at[l])
        at_c()
        ready(l, "f")
        wait()
        step = F // 2
        for j in range(2):
            cols = slice(j * step, (j + 1) * step)
            u = nn(rows_of(Cn.at[l]), W["f"][l, :, :, :, cols].reshape(D, step)) + pack[l, 6:7, cols]
            U[l, :, cols] = u
            Gl[l, :, cols] = gelu(u).astype(BF16)
        ready(l, "p")
        total = scatter_x(lambda c: nt(Gl[l], weight_rows("p", l, c)))
        at_d()
        return (HID[...] + total() + shift(l, 3)) * valid

    def grad_matrix(m, l, left, right):
        span = D // Z

        def step(i, carry):
            cols = pl.ds(pl.multiple_of(i * span, span), span)
            block = tn(left[:, :, cols].reshape(R, span), right())
            G[m][l, i] = block.astype(BF16).reshape(Y, B, sz.width[m])
            return carry

        lax.fori_loop(0, Z, step, 0)

    class Reduce:
        def __init__(self, l, m):
            self.l, self.m = l, m
            g = G[m]
            self.over = copy(g.at[l], SIB[m], sibling, 1 - l)
            self.one_a = [
                copy(g.at[l, :, (y + k) % Y, pl.ds(0, HB)], RA[m].at[k - 1], at_y(k), l)
                for k in far_first(Y)
            ]
            self.one_b = [
                copy(g.at[l, (z + k) % Z, :, pl.ds(HB, HB)], RB[m].at[k - 1], at_z(k), l)
                for k in far_first(Z)
            ]
            self.two_a = [
                copy(g.at[l, (z + k) % Z, y, pl.ds(0, HB)], R2A[m].at[k - 1], at_z(k), l)
                for k in far_first(Z)
            ]
            self.two_b = [
                copy(g.at[l, z, (y + k) % Y, pl.ds(HB, HB)], R2B[m].at[k - 1], at_y(k), l)
                for k in far_first(Y)
            ]

        def send(self):
            self.over.start()

        def add(self):
            g, l, m = G[self.m], self.l, self.m
            self.over.wait_recv()

            def step(i, carry):
                g[l, i] = (g[l, i].astype(F32) + SIB[m][i].astype(F32)).astype(BF16)
                return carry

            lax.fori_loop(0, Z, step, 0)
            for c in self.one_a + self.one_b:
                c.start()

        def middle(self):
            g, l, m = G[self.m], self.l, self.m
            for c in self.one_a:
                c.wait_recv()
            for i in range(Z):
                v = g[l, i, y, 0:HB].astype(F32)
                for k in range(Y - 1):
                    v = v + RA[m][k, i].astype(F32)
                g[l, i, y, 0:HB] = v.astype(BF16)
            for c in self.two_a:
                c.start()
            for c in self.one_b:
                c.wait_recv()
            for i in range(Y):
                v = g[l, z, i, HB:B].astype(F32)
                for k in range(Z - 1):
                    v = v + RB[m][k, i].astype(F32)
                g[l, z, i, HB:B] = v.astype(BF16)
            for c in self.two_b:
                c.start()

        def last(self):
            g, l, m = G[self.m], self.l, self.m
            for c in self.two_a + self.two_b:
                c.wait_recv()
            v = g[l, z, y, 0:HB].astype(F32)
            for k in range(Z - 1):
                v = v + R2A[m][k].astype(F32)
            gout[m][0:HB, :] = v
            v = g[l, z, y, HB:B].astype(F32)
            for k in range(Y - 1):
                v = v + R2B[m][k].astype(F32)
            gout[m][HB:B, :] = v

    reduces = [{m: Reduce(l, m) for m in names} for l in range(2)]

    def task(l, step, *ms):
        def go():
            for m in ms:
                getattr(reduces[l][m], step)()

        on(l, go)

    def hand_over(l, *ms):
        def go():
            for m in ms:
                reduces[l][m].send()

        on(1 - l, go)

    def column_sum(v):
        return jnp.sum(v, axis=0, keepdims=True)

    def layer_backward(l, dY, at_m, at_c, at_h, at_a):
        DM[l, t] = dY.astype(BF16)
        small[l, 5:6, :] = column_sum(dY)
        wait = gather_x(DM.at[l])
        at_m()
        wait()
        step = F // 2
        for j in range(2):
            cols = slice(j * step, (j + 1) * step)
            dg = nn(rows_of(DM.at[l]), W["p"][l, :, :, :, cols].reshape(D, step))
            DU[:, cols] = (dg * gelu_slope(U[l, :, cols])).astype(BF16)
        total = scatter_x(lambda c: nt(DU[...], weight_rows("f", l, c)))
        grad_matrix("p", l, DM.at[l], lambda: Gl[l])
        hand_over(l, "p")
        grad_matrix("f", l, Cn.at[l], lambda: DU[...])
        hand_over(l, "f")
        small[l, 6:7, :] = column_sum(DU[...].astype(F32))
        at_c()
        dc = total()
        dh = dY + norm_back(dc, N2[l], I2[l], gain(l, 1))
        DH[l, t] = dh.astype(BF16)
        wait = gather_x(DH.at[l])
        small[l, 1:2, :] = column_sum(dc * N2[l])
        small[l, 3:4, :] = column_sum(dc)
        small[l, 4:5, :] = column_sum(dh)
        HID[...] = dh
        at_h()
        wait()
        DO[...] = nn(rows_of(DH.at[l]), weight("o", l)).astype(BF16)
        for pair in range(E // (2 * HD)):
            lo = pair * 2 * HD
            q2 = QKV[l, :, lo : lo + 2 * HD]
            k2 = QKV[l, :, E + lo : E + lo + 2 * HD]
            v2 = QKV[l, :, 2 * E + lo : 2 * E + lo + 2 * HD]
            do2 = DO[:, lo : lo + 2 * HD]
            dq = dk = dv = None
            for h in range(2):
                pr = PR[l, pair * 2 + h]
                p = pr.astype(F32)
                dp = nt(do2, half(v2, h))
                ds = (p * (dp - jnp.sum(p * dp, axis=-1, keepdims=True))).astype(BF16)
                parts = (nn(ds, half(k2, h)), tn(ds, half(q2, h)), tn(pr, half(do2, h)))
                if dq is None:
                    dq, dk, dv = parts
                else:
                    dq, dk, dv = dq + parts[0], dk + parts[1], dv + parts[2]
            DQKV[:, lo : lo + 2 * HD] = (dq * factor).astype(BF16)
            DQKV[:, E + lo : E + lo + 2 * HD] = (dk * factor).astype(BF16)
            DQKV[:, 2 * E + lo : 2 * E + lo + 2 * HD] = dv.astype(BF16)
        total = scatter_x(lambda c: nt(DQKV[...], weight_rows("q", l, c)))
        grad_matrix("q", l, A.at[l], lambda: DQKV[...])
        hand_over(l, "q")
        grad_matrix("o", l, DH.at[l], lambda: O[l])
        hand_over(l, "o")
        small[l, 7:8, :] = jnp.zeros((1, D), F32)
        small[l, 7:8, : 3 * E] = column_sum(DQKV[...].astype(F32))
        at_a()
        da = total()
        small[l, 0:1, :] = column_sum(da * N1[l])
        small[l, 2:3, :] = column_sum(da)
        return HID[...] + norm_back(da, N1[l], I1[l], gain(l, 0))

    class Small:
        def __init__(self, l):
            self.l = l
            mine = small.at[l]
            self.over = copy(mine, small_sib, sibling, 1 - l)
            self.x = [copy(mine, small_x.at[k - 1], at_x(k), l) for k in far_first(T)]
            self.y = [copy(small_x.at[T - 1], small_y.at[k - 1], at_y(k), l) for k in far_first(Y)]
            self.z = [copy(small_y.at[Y - 1], small_z.at[k - 1], at_z(k), l) for k in far_first(Z)]

        def begin(self):
            on(1 - self.l, self.over.start)

        def add(self):
            l = self.l
            self.over.wait_recv()
            small[l] = small[l] + small_sib[...]
            for c in self.x:
                c.start()

        def over_x(self):
            for c in self.x:
                c.wait_recv()
            v = small_x[0]
            for k in range(1, T - 1):
                v = v + small_x[k]
            row = lax.broadcasted_iota(jnp.int32, v.shape, 0)
            small_x[T - 1] = small[self.l] + jnp.where(row < 6, v, 0.0)
            for c in self.y:
                c.start()

        def over_y(self):
            for c in self.y:
                c.wait_recv()
            v = small_x[T - 1]
            for k in range(Y - 1):
                v = v + small_y[k]
            small_y[Y - 1] = v
            for c in self.z:
                c.start()

        def over_z(self):
            for c in self.z:
                c.wait_recv()
            v = small_y[Y - 1]
            for k in range(Z - 1):
                v = v + small_z[k]
            small_out[...] = v

    smalls = [Small(l) for l in range(2)]

    def small_task(l, step):
        on(l, getattr(smalls[l], step))

    act_copy = copy(act_send, act_recv, sibling)
    ig_copy = copy(ig_send, ig_recv, sibling)

    def nothing():
        pass

    def f0_a():
        phase(0, "two", "q", "o")

    def f0_b():
        phase(0, "two", "f", "p")
        phase(1, "one", "q", "o", "f", "p")

    def f0_c():
        phase(1, "two", "q")

    def f0_d():
        phase(1, "two", "o", "f", "p")

    y0 = layer_forward(0, x_in[s].astype(F32), f0_a, f0_b, f0_c, f0_d)
    act0 = y0.astype(BF16)

    @pl.when(s == 0)
    def _():
        act_out[0] = act0

    @pl.when(s == 1)
    def _():
        act_send[...] = act0
        act_copy.start()

    y1 = layer_forward(1, act0.astype(F32), nothing, nothing, nothing, nothing)
    act1 = y1.astype(BF16)

    @pl.when(s == 1)
    def _():
        act_out[1] = act1

    @pl.when(s == 0)
    def _():
        act_send[...] = act1
        act_copy.start()

    def b1_h():
        task(1, "add", "p")

    def b1_a():
        task(1, "add", "f")

    ig1 = layer_backward(1, cot_in[s].astype(F32) * valid, nothing, nothing, b1_h, b1_a).astype(BF16)
    smalls[1].begin()

    @pl.when(s == 1)
    def _():
        grad_out[1] = ig1

    @pl.when(s == 0)
    def _():
        ig_send[...] = ig1
        ig_copy.start()

    def b0_m():
        task(1, "add", "q", "o")
        small_task(1, "add")

    def b0_c():
        task(1, "middle", "p", "f")
        small_task(1, "over_x")

    def b0_h():
        task(1, "middle", "q", "o")
        small_task(1, "over_y")
        task(0, "add", "p")

    def b0_a():
        task(1, "last", *names)
        small_task(1, "over_z")
        task(0, "add", "f")
        task(0, "middle", "p")

    ig0 = layer_backward(0, ig1.astype(F32) * valid, b0_m, b0_c, b0_h, b0_a).astype(BF16)
    smalls[0].begin()

    @pl.when(s == 0)
    def _():
        grad_out[0] = ig0

    @pl.when(s == 1)
    def _():
        ig_send[...] = ig0
        ig_copy.start()

    task(0, "add", "q", "o")
    small_task(0, "add")
    task(0, "middle", "f")
    small_task(0, "over_x")
    task(0, "middle", "q", "o")
    small_task(0, "over_y")
    task(0, "last", *names)
    small_task(0, "over_z")

    act_copy.wait_recv()
    act_out[1 - s] = act_recv[...]
    ig_copy.wait_recv()
    grad_out[1 - s] = ig_recv[...]

    groups = {}
    for c, when in drains:
        groups.setdefault(when, []).append(c)
    for when, copies in groups.items():

        def drain(copies=copies):
            for c in copies:
                c.wait_send()

        if when is None:
            drain()
        else:
            on(when, drain)
    assert count[0] <= n_sems, count[0]


def split_dp(n):
    root = int(round(n**0.5))
    return n // root, root


def fused(sz, x, cot, shards, pack, seqs):
    names = sz.names
    Z, Y, T, LR, D, E, F, R = sz.Z, sz.Y, sz.T, sz.LR, sz.D, sz.E, sz.F, sz.R
    wd = sz.width
    n_sems = 400
    vm = pltpu.VMEM
    scratch = (
        [vm((2, Z, Y, sz.B, wd[m]), BF16) for m in names]
        + [vm((2, Z, Y, sz.B, wd[m]), BF16) for m in names]
        + [vm((Z, Y, sz.B, wd[m]), BF16) for m in names]
        + [vm((Y - 1, Z, sz.HB, wd[m]), BF16) for m in names]
        + [vm((Z - 1, Y, sz.HB, wd[m]), BF16) for m in names]
        + [vm((Z - 1, sz.HB, wd[m]), BF16) for m in names]
        + [vm((Y - 1, sz.HB, wd[m]), BF16) for m in names]
        + [vm((2, 8, D), F32)]
        + [vm((2, T, LR, D), BF16)] * 4
        + [
            vm((2, R, 3 * E), BF16),
            vm((2, R, E), BF16),
            vm((2, E // HD, R, R), BF16),
            vm((2, R, F), F32),
            vm((2, R, F), BF16),
        ]
        + [vm((R, F), BF16), vm((R, E), BF16), vm((R, 3 * E), BF16)]
        + [vm((2, LR, D), F32), vm((2, LR, 1), F32), vm((2, LR, D), F32), vm((2, LR, 1), F32)]
        + [vm((LR, D), F32), vm((R, R), F32)]
        + [vm((2, sz.C, T, LR, sz.DC), BF16), vm((8, sz.C, T - 1, LR, sz.DC), BF16)]
        + [
            vm((2, 8, D), F32),
            vm((8, D), F32),
            vm((T, 8, D), F32),
            vm((Y, 8, D), F32),
            vm((Z, 8, D), F32),
        ]
        + [vm((LR, D), BF16)] * 4
        + [pltpu.SemaphoreType.DMA((n_sems,)), pltpu.SemaphoreType.DMA((n_sems,))]
    )
    sds = jax.ShapeDtypeStruct
    out_shape = (
        [sds((2, LR, D), BF16), sds((2, LR, D), BF16)]
        + [sds((sz.B, wd[m]), F32) for m in names]
        + [sds((8, D), F32)]
    )
    spec = pl.BlockSpec(memory_space=pltpu.VMEM)

    def body(*refs):
        kernel_body(sz, n_sems, *refs)

    return pl.pallas_call(
        body,
        out_shape=out_shape,
        in_specs=[spec] * 8,
        out_specs=[spec] * 7,
        scratch_shapes=scratch,
        compiler_params=pltpu.CompilerParams(
            collective_id=0, has_side_effects=True, vmem_limit_bytes=62 << 20
        ),
        name="layers",
    )(x, cot, *shards, pack, seqs)


def per_device(
    inputs,
    cotangent,
    w_qkv,
    b_qkv,
    w_out,
    w_fc,
    b_fc,
    w_proj,
    norm_gains,
    norm_shifts,
    seq_lengths,
    seq_ranks,
    seq_micros,
):
    Z, Y = split_dp(lax.axis_size("dp"))
    T = lax.axis_size("tensor")
    E = w_qkv.shape[3]
    D = inputs.shape[2]
    sz = Sizes(Z, Y, T, inputs.shape[1], D, E, w_fc.shape[2])
    shards = [w_qkv[0].reshape(-1, 3 * E), w_out[0].T, w_fc[0], w_proj[0].T]
    pack = jnp.concatenate(
        [
            norm_gains[0],
            norm_shifts[0],
            jnp.pad(b_fc, ((0, 0), (0, D - b_fc.shape[1]))),
            jnp.pad(b_qkv.reshape(1, 3 * E), ((0, 0), (0, D - 3 * E))),
        ],
        axis=0,
    )
    seqs = jnp.stack([seq_lengths, seq_ranks, seq_micros])
    act, grad, gq, go, gf, gp, small = fused(sz, inputs, cotangent, shards, pack, seqs)
    return (
        act[None],
        grad[None],
        gq.reshape(1, -1, 3, E),
        small[7:8, : 3 * E].reshape(1, 3, E),
        go.T[None],
        gf[None],
        small[6:7, : b_fc.shape[1]],
        gp.T[None],
        small[None, :2],
        small[None, 2:6],
    )


def solution(mesh):
    placed = (
        P(None, ("dp", "tensor"), None),
        P(None, ("dp", "tensor"), None),
        P("section", "dp", None, "tensor"),
        P("section", None, "tensor"),
        P("section", "tensor", "dp"),
        P("section", "dp", "tensor"),
        P("section", "tensor"),
        P("section", "tensor", "dp"),
        P("section", None, None),
        P("section", None, None),
        P(),
        P(),
        P(),
    )
    return jax.shard_map(
        per_device,
        mesh=mesh,
        in_specs=placed,
        out_specs=(
            P("section", None, ("dp", "tensor"), None),
            P("section", None, ("dp", "tensor"), None),
            P("section", "dp", None, "tensor"),
            P("section", None, "tensor"),
            P("section", "tensor", "dp"),
            P("section", "dp", "tensor"),
            P("section", "tensor"),
            P("section", "tensor", "dp"),
            P("section", None, None),
            P("section", None, None),
        ),
        check_vma=False,
    )
```

```python
import jax
import jax.numpy as jnp
from jax import lax
from jax.experimental import pallas as pl
from jax.experimental.pallas import tpu as pltpu
from jax.sharding import PartitionSpec as P

HD = 64
EPS = 1e-05
MESH = pl.DeviceIdType.MESH
F32 = jnp.float32
BF16 = jnp.bfloat16
GELU_A = 0.7978845608028654
GELU_B = 0.044715


def nn(a, b):
    return lax.dot_general(a, b, (((1,), (0,)), ((), ())), preferred_element_type=F32)


def nt(a, b):
    return lax.dot_general(a, b, (((1,), (1,)), ((), ())), preferred_element_type=F32)


def tn(a, b):
    return lax.dot_general(a, b, (((0,), (0,)), ((), ())), preferred_element_type=F32)


def norm(values):
    average = jnp.mean(values, axis=-1, keepdims=True)
    centered = values - average
    inv = lax.rsqrt(jnp.mean(centered * centered, axis=-1, keepdims=True) + EPS)
    return centered * inv, inv


def norm_back(grad, normal, inv, gain):
    scaled = grad * gain
    return inv * (
        scaled
        - jnp.mean(scaled, axis=-1, keepdims=True)
        - normal * jnp.mean(scaled * normal, axis=-1, keepdims=True)
    )


def gelu(u):
    return 0.5 * u * (1.0 + jnp.tanh(GELU_A * (u + GELU_B * u * u * u)))


def gelu_slope(u):
    square = u * u
    t = jnp.tanh(GELU_A * u * (1.0 + GELU_B * square))
    return 0.5 * (1.0 + t) + 0.5 * u * (1.0 - t * t) * (GELU_A * (1.0 + 3.0 * GELU_B * square))


class Sizes:
    def __init__(self, z, y, t, rows, width, heads, hidden):
        self.Z, self.Y, self.T = z, y, t
        self.LR, self.D, self.E, self.F = rows, width, heads, hidden
        self.R = rows * t
        self.C = 2
        self.DC = width // self.C
        self.B = width // (z * y)
        self.HB = self.B // 2
        self.names = ("a", "f", "p")
        self.width = {"a": 4 * heads, "f": hidden, "p": hidden}


def kernel_body(sz, n_sems, *refs):
    names = sz.names
    Z, Y, T, LR, D, E, F, R = sz.Z, sz.Y, sz.T, sz.LR, sz.D, sz.E, sz.F, sz.R
    C, DC, HB, B = sz.C, sz.DC, sz.HB, sz.B
    it = iter(refs)
    x_in, cot_in, wq_in, bq_in, wo_in, wf_in, bf_in, wp_in, gains_in, shifts_in = (
        next(it) for _ in range(10)
    )
    len_in, rank_in, micro_in = next(it), next(it), next(it)
    act_out, grad_out, gq_out, gbq_out, go_out, gf_out, gbf_out, gp_out, gg_out, gs_out = (
        next(it) for _ in range(10)
    )

    def put(m, rows, v):
        if m == "a":
            for c in range(3):
                gq_out[c, rows, :] = v[:, c * E : (c + 1) * E]
            go_out[rows, :] = v[:, 3 * E :]
        else:
            (gf_out if m == "f" else gp_out)[rows, :] = v

    W = {m: next(it) for m in names}
    G = {m: next(it) for m in names}
    SIB = {m: next(it) for m in names}
    RA = {m: next(it) for m in names}
    R2 = {m: next(it) for m in names}
    FIN = {m: next(it) for m in names}
    pack = next(it)
    A, Cn, DM, DH = next(it), next(it), next(it), next(it)
    QKV, O, PR, U, Gl = next(it), next(it), next(it), next(it), next(it)
    DU, DO, DQKV = next(it), next(it), next(it)
    N1, I1, N2, I2 = next(it), next(it), next(it), next(it)
    HID = next(it)
    MASK = next(it)
    stage, recv = next(it), next(it)
    small, small_sib, small_x, small_y, small_z = next(it), next(it), next(it), next(it), next(it)
    act_send, act_recv, ig_send, ig_recv = next(it), next(it), next(it), next(it)
    send_sem, recv_sem = next(it), next(it)

    s = lax.axis_index("section")
    d = lax.axis_index("dp")
    t = lax.axis_index("tensor")
    z = d // Y
    y = d % Y
    count = [0]
    shared = {}
    drains = []

    class Move:
        def __init__(self, src, dst, device, when=None, key=None):
            i = shared.get(key)
            if i is None:
                i = count[0]
                count[0] += 1
                if key is not None:
                    shared[key] = i
            self.when = when
            self.made = pltpu.make_async_remote_copy(
                src_ref=src,
                dst_ref=dst,
                send_sem=send_sem.at[i],
                recv_sem=recv_sem.at[i],
                device_id=device,
                device_id_type=MESH,
            )

        def start(self):
            self.made.start()
            if self not in drains:
                drains.append(self)

        def wait_recv(self):
            self.made.wait_recv()

        def wait_send(self):
            self.made.wait_send()

    copy = Move

    def at_x(k):
        return (s, d, (t + k) % T)

    def at_y(k):
        return (s, z * Y + (y + k) % Y, t)

    def at_z(k):
        return (s, ((z + k) % Z) * Y + y, t)

    sibling = (1 - s, d, t)

    def far_first(n):
        return sorted(range(1, n), key=lambda k: -min(k, n - k))

    barrier = pltpu.get_barrier_semaphore()
    peers = (
        [at_x(k) for k in range(1, T)]
        + [at_y(k) for k in range(1, Y)]
        + [at_z(k) for k in range(1, Z)]
        + [sibling]
    )
    for p in peers:
        pl.semaphore_signal(barrier, inc=1, device_id=p, device_id_type=MESH)

    for c in range(3):
        W["a"][s, z, y, :, c * E : (c + 1) * E] = wq_in[c]
        pack[s, 7:8, c * E : (c + 1) * E] = bq_in[:, c * E : (c + 1) * E]
    W["a"][s, z, y, :, 3 * E :] = wo_in[...]
    W["f"][s, z, y] = wf_in[...]
    W["p"][s, z, y] = wp_in[...]
    pack[s, 0:2, :] = gains_in[...]
    pack[s, 2:6, :] = shifts_in[...]
    pack[s, 6:7, :F] = bf_in[...]
    pl.semaphore_wait(barrier, len(peers))

    pack_copy = copy(pack.at[s], pack.at[s], sibling)
    pack_copy.start()

    def on(core, f):
        pl.when(s == core)(f)

    class Gather:
        def __init__(self, l, m):
            w = W[m]
            self.l = l
            half = [pl.ds(0, HB), pl.ds(HB, HB)]

            def same(view, device, when, *key):
                return copy(view, view, device, when, ("gather", l, m) + key)

            give = w.at[l, z, y, half[1 - l]]
            self.zero = same(give, sibling, l, 0)
            zs = [(z + k) % Z for k in range(Z)]
            ys = [(y + k) % Y for k in range(Y)]
            self.one, self.two, self.far, self.over = [], [], [], []
            for h in range(2):
                own = w.at[l, z, y, half[h]]
                if h == 0:
                    n, m_, at_one, at_two, ring = Y, Z, at_y, at_z, zs

                    def strip(i, lo=0, size=Y, ring=ring, h=h):
                        return w.at[l, ring[i], pl.ds(lo, size), half[h]]

                else:
                    n, m_, at_one, at_two, ring = Z, Y, at_z, at_y, ys

                    def strip(i, lo=0, size=Z, ring=ring, h=h):
                        return w.at[l, pl.ds(lo, size), ring[i], half[h]]

                self.one.append([same(own, at_one(k), h, 1, k) for k in far_first(n)])
                self.two.append({k: same(strip(0), at_two(k), h, 2, k) for k in (1, m_ - 1)})
                self.far.append(
                    {
                        1: same(strip(m_ - 1, 0, n // 2), at_two(1), h, 3, 1),
                        m_ - 1: same(strip(1, n // 2, n // 2), at_two(m_ - 1), h, 3, 2),
                    }
                )
                if h == l:
                    first = [same(strip(0), sibling, h, 4, 0)]
                else:
                    at = [(z, (y + k) % Y) if h == 0 else ((z + k) % Z, y) for k in range(1, n)]
                    first = [
                        same(w.at[l, zz, yy, half[h]], sibling, h, 4, 0, k)
                        for k, (zz, yy) in enumerate(at)
                    ]
                self.over.append([first] + [[same(strip(i), sibling, h, 4, i)] for i in range(1, m_)])

        def s0(self):
            on(self.l, self.zero.start)

        def s1(self, h):
            if h != self.l:
                self.zero.wait_recv()
            for c in self.one[h]:
                c.start()

        def s2(self, h):
            for c in self.one[h]:
                c.wait_recv()
            for c in self.two[h].values():
                c.start()
            for c in self.over[h][0]:
                c.start()

        def s3(self, h):
            for k, c in self.two[h].items():
                c.wait_recv()
                self.far[h][k].start()
                self.over[h][1 if k != 1 else len(self.over[h]) - 1][0].start()

        def s4(self, h):
            for c in self.far[h].values():
                c.wait_recv()
            self.over[h][2][0].start()

        def s5(self, h):
            for group in self.over[1 - h]:
                for c in group:
                    c.wait_recv()

    gathers = [{m: Gather(l, m) for m in names} for l in range(2)]

    def phase(l, *steps):
        for h in range(2):

            def go(h=h):
                for one in steps:
                    getattr(gathers[l][one[0]], one[1:])(h)

            on(h, go)

    def ready(l, m):
        phase(l, m + "s5")

    for l in range(2):
        for m in names:
            gathers[l][m].s0()
    phase(0, "as1", "fs1", "ps1")

    lengths, ranks, micros = (r[...].astype(F32) for r in (len_in, rank_in, micro_in))
    n_seq = lengths.shape[1]
    mine_row = jnp.logical_and(ranks == d.astype(F32), micros == s.astype(F32))
    taken_row = jnp.where(mine_row, lengths, 0.0)
    i0 = lax.broadcasted_iota(jnp.int32, (n_seq, n_seq), 0)
    i1 = lax.broadcasted_iota(jnp.int32, (n_seq, n_seq), 1)
    taken_col = jnp.sum(jnp.where(i0 == i1, taken_row, 0.0), axis=1, keepdims=True)
    ends_col = jnp.sum(jnp.where(i1 <= i0, taken_row, 0.0), axis=1, keepdims=True)
    ends_row = jnp.sum(jnp.where(i0 <= i1, taken_col, 0.0), axis=0, keepdims=True)
    number_row = lax.broadcasted_iota(jnp.int32, (1, n_seq), 1).astype(F32) + 1.0
    number_col = lax.broadcasted_iota(jnp.int32, (n_seq, 1), 0).astype(F32) + 1.0

    def column_labels(rows, first):
        places = (lax.broadcasted_iota(jnp.int32, (rows, n_seq), 0) + first).astype(F32)
        inside = jnp.logical_and(places >= ends_row - taken_row, places < ends_row)
        return jnp.sum(jnp.where(inside, number_row, 0.0), axis=1, keepdims=True)

    label_col = column_labels(R, 0)
    places = lax.broadcasted_iota(jnp.int32, (n_seq, R), 1).astype(F32)
    inside = jnp.logical_and(places >= ends_col - taken_col, places < ends_col)
    label_row = jnp.sum(jnp.where(inside, number_col, 0.0), axis=0, keepdims=True)
    r0 = lax.broadcasted_iota(jnp.int32, (R, R), 0)
    r1 = lax.broadcasted_iota(jnp.int32, (R, R), 1)
    same = jnp.logical_and(label_col == label_row, label_col > 0.5)
    visible = jnp.logical_or(jnp.logical_and(same, r1 <= r0), r0 == r1)
    MASK[...] = jnp.where(visible, 1.0, 0.0)
    valid = jnp.where(column_labels(LR, t * LR) > 0.5, 1.0, 0.0)

    pack_copy.wait_recv()

    def gain(l, i):
        return pack[l, i : i + 1, :]

    def shift(l, i):
        return pack[l, 2 + i : 3 + i, :]

    turns = [[], []]
    turn = [0]

    def next_turn():
        slot = turn[0] % 2
        turn[0] += 1
        for c in turns[slot]:
            c.wait_send()
            drains.remove(c)
        turns[slot] = []
        return slot

    def gather_x(buf):
        slot = next_turn()
        copies = [copy(buf.at[t], buf.at[t], at_x(k), None, ("x", slot, 0, k)) for k in far_first(T)]
        for c in copies:
            c.start()
        turns[slot] = copies

        def wait():
            for c in copies:
                c.wait_recv()

        return wait

    scatters = [0]

    def scatter_x(part):
        slot = next_turn()
        number = scatters[0]
        scatters[0] += 1
        copies = []
        for c in range(C):
            stage[number % 2, c] = part(c).astype(BF16).reshape(T, LR, DC)
            for k in far_first(T):
                one = copy(
                    stage.at[number % 2, c, (t + k) % T],
                    recv.at[number, c, k - 1],
                    at_x(k),
                    None,
                    ("x", slot, c, k),
                )
                one.start()
                copies.append(one)
        turns[slot] = copies

        def total():
            for c in copies:
                c.wait_recv()
            out = []
            for c in range(C):
                v = stage[number % 2, c, t].astype(F32)
                for k in range(1, T):
                    v = v + recv[number, c, k - 1].astype(F32)
                out.append(v)
            return jnp.concatenate(out, axis=1)

        return total

    lanes = lax.broadcasted_iota(jnp.int32, (R, 2 * HD), 1)

    def half(v, h):
        keep = lanes < HD if h == 0 else lanes >= HD
        return jnp.where(keep, v, jnp.zeros_like(v))

    factor = HD ** (-0.5)

    def rows_of(buf):
        return buf[...].reshape(R, D)

    parts_of = {"q": ("a", 0, 3 * E), "o": ("a", 3 * E, 4 * E), "f": ("f", 0, F), "p": ("p", 0, F)}

    def weight(m, l):
        w, lo, hi = parts_of[m]
        return W[w][l, :, :, :, lo:hi].reshape(D, hi - lo)

    def weight_rows(m, l, c):
        w, lo, hi = parts_of[m]
        span = Z // C
        return W[w][l, c * span : (c + 1) * span, :, :, lo:hi].reshape(DC, hi - lo)

    def layer_forward(l, X, at_a, at_q, at_b, at_c, at_d):
        n1, inv1 = norm(X)
        N1[l] = n1
        I1[l] = inv1
        A[l, t] = (n1 * gain(l, 0) + shift(l, 0)).astype(BF16)
        wait = gather_x(A.at[l])
        at_a()
        ready(l, "a")
        wait()
        bias = pack[l, 7:8, : 3 * E]
        QKV[l] = (nn(rows_of(A.at[l]), weight("q", l)) + bias).astype(BF16)
        at_q()
        for pair in range(E // (2 * HD)):
            lo = pair * 2 * HD
            q2 = QKV[l, :, lo : lo + 2 * HD]
            k2 = QKV[l, :, E + lo : E + lo + 2 * HD]
            v2 = QKV[l, :, 2 * E + lo : 2 * E + lo + 2 * HD]
            o2 = None
            for h in range(2):
                S = nt(q2, half(k2, h)) * factor
                S = jnp.where(MASK[...] > 0.5, S, -1e30)
                e = jnp.exp(S - jnp.max(S, axis=-1, keepdims=True))
                pr = (e / jnp.sum(e, axis=-1, keepdims=True)).astype(BF16)
                PR[l, pair * 2 + h] = pr
                part = nn(pr, half(v2, h))
                o2 = part if o2 is None else o2 + part
            O[l, :, lo : lo + 2 * HD] = o2.astype(BF16)
        total = scatter_x(lambda c: nt(O[l], weight_rows("o", l, c)))
        at_b()
        hidden = X + total() + shift(l, 2)
        n2, inv2 = norm(hidden)
        N2[l] = n2
        I2[l] = inv2
        HID[...] = hidden
        Cn[l, t] = (n2 * gain(l, 1) + shift(l, 1)).astype(BF16)
        wait = gather_x(Cn.at[l])
        at_c()
        ready(l, "f")
        wait()
        step = F // 2
        for j in range(2):
            cols = slice(j * step, (j + 1) * step)
            u = nn(rows_of(Cn.at[l]), W["f"][l, :, :, :, cols].reshape(D, step)) + pack[l, 6:7, cols]
            U[l, :, cols] = u
            Gl[l, :, cols] = gelu(u).astype(BF16)
        ready(l, "p")
        total = scatter_x(lambda c: nt(Gl[l], weight_rows("p", l, c)))
        at_d()
        return (HID[...] + total() + shift(l, 3)) * valid

    def grad_matrix(m, l, left, right):
        span = D // Z
        w, lo, hi = parts_of[m]

        def step(i, carry):
            cols = pl.ds(pl.multiple_of(i * span, span), span)
            block = tn(left[:, :, cols].reshape(R, span), right())
            G[w][l, i, :, :, lo:hi] = block.astype(BF16).reshape(Y, B, hi - lo)
            return carry

        lax.fori_loop(0, Z, step, 0)

    class Reduce:
        def __init__(self, l, m):
            self.l, self.m = l, m
            g = G[m]
            half = [pl.ds(0, HB), pl.ds(HB, HB)]
            self.over = [
                copy(g.at[l, :, :, half[1 - h]], SIB[m].at[l], sibling, h, (l, m, 0)) for h in range(2)
            ]
            self.one = [
                [
                    copy(g.at[l, :, (y + k) % Y, half[0]], RA[m].at[l, k - 1], at_y(k), 0, (l, m, 1, k))
                    for k in far_first(Y)
                ],
                [
                    copy(g.at[l, (z + k) % Z, :, half[1]], RA[m].at[l, k - 1], at_z(k), 1, (l, m, 1, k))
                    for k in far_first(Z)
                ],
            ]
            self.two = [
                [
                    copy(g.at[l, (z + k) % Z, y, half[0]], R2[m].at[l, k - 1], at_z(k), 0, (l, m, 2, k))
                    for k in far_first(Z)
                ],
                [
                    copy(g.at[l, z, (y + k) % Y, half[1]], R2[m].at[l, k - 1], at_y(k), 1, (l, m, 2, k))
                    for k in far_first(Y)
                ],
            ]
            self.back = copy(FIN[m].at[0], FIN[m].at[1], sibling, 1 - l)

        def r0(self, h):
            self.over[h].start()

        def r1(self, h):
            g, l, m = G[self.m], self.l, self.m
            rows = slice(h * HB, h * HB + HB)
            self.over[1 - h].wait_recv()

            def step(i, carry):
                g[l, i, :, rows] = (g[l, i, :, rows].astype(F32) + SIB[m][l, i].astype(F32)).astype(BF16)
                return carry

            lax.fori_loop(0, Z, step, 0)
            for c in self.one[h]:
                c.start()

        def r2(self, h):
            g, l, m = G[self.m], self.l, self.m
            rows = slice(h * HB, h * HB + HB)
            for c in self.one[h]:
                c.wait_recv()
            n = len(self.one[h])
            for i in range(n + 1):
                at = (l, i, y, rows) if h == 0 else (l, z, i, rows)
                v = g[at].astype(F32)
                for k in range(n):
                    v = v + RA[m][l, k, i].astype(F32)
                g[at] = v.astype(BF16)
            for c in self.two[h]:
                c.start()

        def r3(self, h):
            g, l, m = G[self.m], self.l, self.m
            rows = slice(h * HB, h * HB + HB)
            for c in self.two[h]:
                c.wait_recv()
            v = g[l, z, y, rows].astype(F32)
            for k in range(len(self.two[h])):
                v = v + R2[m][l, k].astype(F32)
            if h == l:
                put(m, rows, v)
            else:
                FIN[m][0] = v
                self.back.start()

        def r4(self, h):
            if h == self.l:
                self.back.wait_recv()
                put(self.m, slice((1 - h) * HB, (2 - h) * HB), FIN[self.m][1])

    reduces = [{m: Reduce(l, m) for m in names} for l in range(2)]

    def task(l, *steps):
        for h in range(2):

            def go(h=h):
                for one in steps:
                    getattr(reduces[l][one[0]], one[1:])(h)

            on(h, go)

    def hand_over(l, m):
        task(l, m + "r0")

    def column_sum(v):
        return jnp.sum(v, axis=0, keepdims=True)

    def layer_backward(l, dY, at_m, at_c, at_h, at_a):
        DM[l, t] = dY.astype(BF16)
        small[l, 5:6, :] = column_sum(dY)
        wait = gather_x(DM.at[l])
        at_m()
        wait()
        step = F // 2
        for j in range(2):
            cols = slice(j * step, (j + 1) * step)
            dg = nn(rows_of(DM.at[l]), W["p"][l, :, :, :, cols].reshape(D, step))
            DU[:, cols] = (dg * gelu_slope(U[l, :, cols])).astype(BF16)
        total = scatter_x(lambda c: nt(DU[...], weight_rows("f", l, c)))
        grad_matrix("p", l, DM.at[l], lambda: Gl[l])
        hand_over(l, "p")
        grad_matrix("f", l, Cn.at[l], lambda: DU[...])
        hand_over(l, "f")
        small[l, 6:7, :] = column_sum(DU[...].astype(F32))
        at_c()
        dc = total()
        dh = dY + norm_back(dc, N2[l], I2[l], gain(l, 1))
        DH[l, t] = dh.astype(BF16)
        wait = gather_x(DH.at[l])
        small[l, 1:2, :] = column_sum(dc * N2[l])
        small[l, 3:4, :] = column_sum(dc)
        small[l, 4:5, :] = column_sum(dh)
        HID[...] = dh
        at_h()
        wait()
        DO[...] = nn(rows_of(DH.at[l]), weight("o", l)).astype(BF16)
        for pair in range(E // (2 * HD)):
            lo = pair * 2 * HD
            q2 = QKV[l, :, lo : lo + 2 * HD]
            k2 = QKV[l, :, E + lo : E + lo + 2 * HD]
            v2 = QKV[l, :, 2 * E + lo : 2 * E + lo + 2 * HD]
            do2 = DO[:, lo : lo + 2 * HD]
            dq = dk = dv = None
            for h in range(2):
                pr = PR[l, pair * 2 + h]
                p = pr.astype(F32)
                dp = nt(do2, half(v2, h))
                ds = (p * (dp - jnp.sum(p * dp, axis=-1, keepdims=True))).astype(BF16)
                parts = (nn(ds, half(k2, h)), tn(ds, half(q2, h)), tn(pr, half(do2, h)))
                if dq is None:
                    dq, dk, dv = parts
                else:
                    dq, dk, dv = dq + parts[0], dk + parts[1], dv + parts[2]
            DQKV[:, lo : lo + 2 * HD] = (dq * factor).astype(BF16)
            DQKV[:, E + lo : E + lo + 2 * HD] = (dk * factor).astype(BF16)
            DQKV[:, 2 * E + lo : 2 * E + lo + 2 * HD] = dv.astype(BF16)
        total = scatter_x(lambda c: nt(DQKV[...], weight_rows("q", l, c)))
        grad_matrix("q", l, A.at[l], lambda: DQKV[...])
        grad_matrix("o", l, DH.at[l], lambda: O[l])
        hand_over(l, "a")
        small[l, 7:8, :] = jnp.zeros((1, D), F32)
        small[l, 7:8, : 3 * E] = column_sum(DQKV[...].astype(F32))
        at_a()
        da = total()
        small[l, 0:1, :] = column_sum(da * N1[l])
        small[l, 2:3, :] = column_sum(da)
        return HID[...] + norm_back(da, N1[l], I1[l], gain(l, 0))

    class Small:
        def __init__(self, l):
            self.l = l
            mine = small.at[l]
            self.over = copy(mine, small_sib, sibling, 1 - l, "small")
            self.x = [copy(mine, small_x.at[k - 1], at_x(k), l, ("small", 0, k)) for k in far_first(T)]
            self.y = [copy(small_x.at[T - 1], small_y.at[k - 1], at_y(k), l, ("small", 1, k)) for k in far_first(Y)]
            self.z = [copy(small_y.at[Y - 1], small_z.at[k - 1], at_z(k), l, ("small", 2, k)) for k in far_first(Z)]

        def begin(self):
            on(1 - self.l, self.over.start)

        def add(self):
            l = self.l
            self.over.wait_recv()
            small[l] = small[l] + small_sib[...]
            for c in self.x:
                c.start()

        def over_x(self):
            for c in self.x:
                c.wait_recv()
            v = small_x[0]
            for k in range(1, T - 1):
                v = v + small_x[k]
            row = lax.broadcasted_iota(jnp.int32, v.shape, 0)
            small_x[T - 1] = small[self.l] + jnp.where(row < 6, v, 0.0)
            for c in self.y:
                c.start()

        def over_y(self):
            for c in self.y:
                c.wait_recv()
            v = small_x[T - 1]
            for k in range(Y - 1):
                v = v + small_y[k]
            small_y[Y - 1] = v
            for c in self.z:
                c.start()

        def over_z(self):
            for c in self.z:
                c.wait_recv()
            v = small_y[Y - 1]
            for k in range(Z - 1):
                v = v + small_z[k]
            gg_out[...] = v[0:2]
            gs_out[...] = v[2:6]
            gbf_out[...] = v[6:7, :F]
            gbq_out[...] = v[7:8, : 3 * E]

    smalls = [Small(l) for l in range(2)]

    def small_task(l, step):
        on(l, getattr(smalls[l], step))

    act_copy = copy(act_send, act_recv, sibling)
    ig_copy = copy(ig_send, ig_recv, sibling)

    def f0_a():
        phase(0, "as2", "fs2", "as3", "ps2", "as4")

    def f0_q():
        phase(0, "fs3")

    def f0_b():
        phase(0, "ps3", "fs4")
        phase(1, "as1", "fs1", "ps1")

    def f0_c():
        phase(0, "ps4")
        phase(1, "as2", "fs2", "ps2")

    def f0_d():
        phase(1, "as3", "fs3")

    def f1_a():
        phase(1, "ps3", "as4")

    def f1_b():
        phase(1, "fs4", "ps4")

    def nothing():
        pass

    y0 = layer_forward(0, x_in[s].astype(F32), f0_a, f0_q, f0_b, f0_c, f0_d)
    act0 = y0.astype(BF16)

    @pl.when(s == 0)
    def _():
        act_out[0] = act0

    @pl.when(s == 1)
    def _():
        act_send[...] = act0
        act_copy.start()

    y1 = layer_forward(1, act0.astype(F32), f1_a, nothing, f1_b, nothing, nothing)
    act1 = y1.astype(BF16)

    @pl.when(s == 1)
    def _():
        act_out[1] = act1

    @pl.when(s == 0)
    def _():
        act_send[...] = act1
        act_copy.start()

    def b1_h():
        task(1, "pr1")

    def b1_a():
        task(1, "fr1", "pr2")

    ig1 = layer_backward(1, cot_in[s].astype(F32) * valid, nothing, nothing, b1_h, b1_a).astype(BF16)
    smalls[1].begin()

    @pl.when(s == 1)
    def _():
        grad_out[1] = ig1

    @pl.when(s == 0)
    def _():
        ig_send[...] = ig1
        ig_copy.start()

    def b0_m():
        task(1, "ar1", "fr2")
        small_task(1, "add")

    def b0_c():
        task(1, "ar2", "pr3")
        small_task(1, "over_x")

    def b0_h():
        task(1, "fr3")
        small_task(1, "over_y")
        task(0, "pr1")

    def b0_a():
        task(0, "fr1", "pr2")
        task(1, "ar3")
        small_task(1, "over_z")

    ig0 = layer_backward(0, ig1.astype(F32) * valid, b0_m, b0_c, b0_h, b0_a).astype(BF16)
    smalls[0].begin()

    @pl.when(s == 0)
    def _():
        grad_out[0] = ig0

    @pl.when(s == 1)
    def _():
        ig_send[...] = ig0
        ig_copy.start()

    task(0, "ar1", "fr2")
    small_task(0, "add")
    small_task(0, "over_x")
    task(0, "pr3", "ar2")
    small_task(0, "over_y")
    task(0, "fr3", "ar3")
    small_task(0, "over_z")
    for l in range(2):
        task(l, *(m + "r4" for m in names))

    act_copy.wait_recv()
    act_out[1 - s] = act_recv[...]
    ig_copy.wait_recv()
    grad_out[1 - s] = ig_recv[...]

    groups = {}
    for c in drains:
        groups.setdefault(c.when, []).append(c)
    for when, copies in groups.items():

        def drain(copies=copies):
            for c in copies:
                c.wait_send()

        if when is None:
            drain()
        else:
            on(when, drain)
    assert count[0] <= n_sems, count[0]


def split_dp(n):
    root = int(round(n**0.5))
    return n // root, root


def fused(sz, arrays, out_shape):
    names = sz.names
    Z, Y, T, LR, D, E, F, R = sz.Z, sz.Y, sz.T, sz.LR, sz.D, sz.E, sz.F, sz.R
    wd = sz.width
    n_sems = 168
    vm = pltpu.VMEM
    scratch = (
        [vm((2, Z, Y, sz.B, wd[m]), BF16) for m in names]
        + [vm((2, Z, Y, sz.B, wd[m]), BF16) for m in names]
        + [vm((2, Z, Y, sz.HB, wd[m]), BF16) for m in names]
        + [vm((2, Y - 1, Z, sz.HB, wd[m]), BF16) for m in names]
        + [vm((2, Z - 1, sz.HB, wd[m]), BF16) for m in names]
        + [vm((2, sz.HB, wd[m]), F32) for m in names]
        + [vm((2, 8, D), F32)]
        + [vm((2, T, LR, D), BF16)] * 4
        + [
            vm((2, R, 3 * E), BF16),
            vm((2, R, E), BF16),
            vm((2, E // HD, R, R), BF16),
            vm((2, R, F), F32),
            vm((2, R, F), BF16),
        ]
        + [vm((R, F), BF16), vm((R, E), BF16), vm((R, 3 * E), BF16)]
        + [vm((2, LR, D), F32), vm((2, LR, 1), F32), vm((2, LR, D), F32), vm((2, LR, 1), F32)]
        + [vm((LR, D), F32), vm((R, R), F32)]
        + [vm((2, sz.C, T, LR, sz.DC), BF16), vm((8, sz.C, T - 1, LR, sz.DC), BF16)]
        + [
            vm((2, 8, D), F32),
            vm((8, D), F32),
            vm((T, 8, D), F32),
            vm((Y, 8, D), F32),
            vm((Z, 8, D), F32),
        ]
        + [vm((LR, D), BF16)] * 4
        + [pltpu.SemaphoreType.DMA((n_sems,)), pltpu.SemaphoreType.DMA((n_sems,))]
    )
    spec = pl.BlockSpec(memory_space=pltpu.VMEM)

    def body(*refs):
        kernel_body(sz, n_sems, *refs)

    return pl.pallas_call(
        body,
        out_shape=out_shape,
        in_specs=[spec] * len(arrays),
        out_specs=[spec] * len(out_shape),
        scratch_shapes=scratch,
        compiler_params=pltpu.CompilerParams(
            collective_id=0, has_side_effects=True, vmem_limit_bytes=62 << 20
        ),
        name="layers",
    )(*arrays)


def hand_out(arrays):
    n = len(arrays)

    def body(*refs):
        sems = refs[2 * n]
        copies = [pltpu.make_async_copy(refs[i], refs[n + i], sems.at[i]) for i in range(n)]
        for c in copies:
            c.start()
        for c in copies:
            c.wait()

    return pl.pallas_call(
        body,
        out_shape=[jax.ShapeDtypeStruct(a.shape, a.dtype) for a in arrays],
        in_specs=[pl.BlockSpec(memory_space=pltpu.VMEM)] * n,
        out_specs=[pl.BlockSpec(memory_space=pl.ANY)] * n,
        scratch_shapes=[pltpu.SemaphoreType.DMA((n,))],
        name="hand_out",
    )(*arrays)


def per_device(*arrays):
    inputs, cotangent, w_qkv, b_qkv, w_out, w_fc, b_fc, w_proj, gains, shifts = arrays[:10]
    Z, Y = split_dp(lax.axis_size("dp"))
    T = lax.axis_size("tensor")
    E = w_qkv.shape[3]
    sz = Sizes(Z, Y, T, inputs.shape[1], inputs.shape[2], E, w_fc.shape[2])
    params = [
        w_qkv[0].transpose(1, 0, 2),
        b_qkv.reshape(1, 3 * E),
        w_out[0].T,
        w_fc[0],
        b_fc,
        w_proj[0].T,
        gains[0],
        shifts[0],
    ]
    seqs = [a.reshape(1, -1) for a in arrays[10:]]
    out_shape = [jax.ShapeDtypeStruct(inputs.shape, BF16)] * 2 + [
        jax.ShapeDtypeStruct(a.shape, F32) for a in params
    ]
    act, grad, gq, gbq, go, gf, gbf, gp, gg, gs = hand_out(
        fused(sz, [inputs, cotangent] + params + seqs, out_shape)
    )
    return (
        act[None],
        grad[None],
        gq.transpose(1, 0, 2)[None],
        gbq.reshape(1, 3, E),
        go.T[None],
        gf[None],
        gbf,
        gp.T[None],
        gg[None],
        gs[None],
    )


def solution(mesh):
    placed = (
        P(None, ("dp", "tensor"), None),
        P(None, ("dp", "tensor"), None),
        P("section", "dp", None, "tensor"),
        P("section", None, "tensor"),
        P("section", "tensor", "dp"),
        P("section", "dp", "tensor"),
        P("section", "tensor"),
        P("section", "tensor", "dp"),
        P("section", None, None),
        P("section", None, None),
        P(),
        P(),
        P(),
    )
    return jax.shard_map(
        per_device,
        mesh=mesh,
        in_specs=placed,
        out_specs=(
            P("section", None, ("dp", "tensor"), None),
            P("section", None, ("dp", "tensor"), None),
            P("section", "dp", None, "tensor"),
            P("section", None, "tensor"),
            P("section", "tensor", "dp"),
            P("section", "dp", "tensor"),
            P("section", "tensor"),
            P("section", "tensor", "dp"),
            P("section", None, None),
            P("section", None, None),
        ),
        check_vma=False,
    )
```

```python
import jax
import jax.numpy as jnp
from jax import lax
from jax.experimental import pallas as pl
from jax.experimental.pallas import tpu as pltpu
from jax.sharding import PartitionSpec as P

HD = 64
EPS = 1e-05
MESH = pl.DeviceIdType.MESH
F32 = jnp.float32
BF16 = jnp.bfloat16
GELU_A = 0.7978845608028654
GELU_B = 0.044715


def nn(a, b):
    return lax.dot_general(a, b, (((1,), (0,)), ((), ())), preferred_element_type=F32)


def nt(a, b):
    return lax.dot_general(a, b, (((1,), (1,)), ((), ())), preferred_element_type=F32)


def tn(a, b):
    return lax.dot_general(a, b, (((0,), (0,)), ((), ())), preferred_element_type=F32)


def norm(values):
    average = jnp.mean(values, axis=-1, keepdims=True)
    centered = values - average
    inv = lax.rsqrt(jnp.mean(centered * centered, axis=-1, keepdims=True) + EPS)
    return centered * inv, inv


def norm_back(grad, normal, inv, gain):
    scaled = grad * gain
    return inv * (
        scaled
        - jnp.mean(scaled, axis=-1, keepdims=True)
        - normal * jnp.mean(scaled * normal, axis=-1, keepdims=True)
    )


def gelu(u):
    return 0.5 * u * (1.0 + jnp.tanh(GELU_A * (u + GELU_B * u * u * u)))


def gelu_slope(u):
    square = u * u
    t = jnp.tanh(GELU_A * u * (1.0 + GELU_B * square))
    return 0.5 * (1.0 + t) + 0.5 * u * (1.0 - t * t) * (GELU_A * (1.0 + 3.0 * GELU_B * square))


class Sizes:
    def __init__(self, z, y, t, rows, width, heads, hidden):
        self.Z, self.Y, self.T = z, y, t
        self.LR, self.D, self.E, self.F = rows, width, heads, hidden
        self.R = rows * t
        self.HR = rows // 2
        self.B = width // (z * y)
        self.HB = self.B // 2
        self.names = ("a", "f", "p")
        self.width = {"a": 4 * heads, "f": hidden, "p": hidden}


def kernel_body(sz, n_sems, *refs):
    names = sz.names
    Z, Y, T, LR, D, E, F, R = sz.Z, sz.Y, sz.T, sz.LR, sz.D, sz.E, sz.F, sz.R
    HR, HB, B = sz.HR, sz.HB, sz.B
    it = iter(refs)
    x_in, cot_in, wq_in, bq_in, wo_in, wf_in, bf_in, wp_in, gains_in, shifts_in = (
        next(it) for _ in range(10)
    )
    len_in, rank_in, micro_in = next(it), next(it), next(it)
    act_out, grad_out, gq_out, gbq_out, go_out, gf_out, gbf_out, gp_out, gg_out, gs_out = (
        next(it) for _ in range(10)
    )

    def put(m, rows, v):
        if m == "a":
            for c in range(3):
                gq_out[c, rows, :] = v[:, c * E : (c + 1) * E]
            go_out[rows, :] = v[:, 3 * E :]
        else:
            (gf_out if m == "f" else gp_out)[rows, :] = v

    W = {m: next(it) for m in names}
    G = {m: next(it) for m in names}
    SIB = {m: next(it) for m in names}
    RA = {m: next(it) for m in names}
    R2 = {m: next(it) for m in names}
    FIN = {m: next(it) for m in names}
    pack = next(it)
    A, Cn, DM, DH = next(it), next(it), next(it), next(it)
    QKV, O, PR, U, Gl = next(it), next(it), next(it), next(it), next(it)
    DU, DO, DQKV = next(it), next(it), next(it)
    N1, I1, N2, I2 = next(it), next(it), next(it), next(it)
    HID, DYS = next(it), next(it)
    MASK = next(it)
    stage, recv = next(it), next(it)
    small, small_sib, small_x, small_y, small_z = next(it), next(it), next(it), next(it), next(it)
    act_send, act_recv, ig_send, ig_recv = next(it), next(it), next(it), next(it)
    send_sem, recv_sem = next(it), next(it)

    s = lax.axis_index("section")
    d = lax.axis_index("dp")
    t = lax.axis_index("tensor")
    z = d // Y
    y = d % Y
    count = [0]
    shared = {}
    drains = []

    class Move:
        def __init__(self, src, dst, device, when=None, key=None):
            i = shared.get(key)
            if i is None:
                i = count[0]
                count[0] += 1
                if key is not None:
                    shared[key] = i
            self.when = when
            self.made = pltpu.make_async_remote_copy(
                src_ref=src,
                dst_ref=dst,
                send_sem=send_sem.at[i],
                recv_sem=recv_sem.at[i],
                device_id=device,
                device_id_type=MESH,
            )

        def start(self):
            self.made.start()
            if self not in drains:
                drains.append(self)

        def wait_recv(self):
            self.made.wait_recv()

        def wait_send(self):
            self.made.wait_send()

    copy = Move

    def at_x(k):
        return (s, d, (t + k) % T)

    def at_y(k):
        return (s, z * Y + (y + k) % Y, t)

    def at_z(k):
        return (s, ((z + k) % Z) * Y + y, t)

    sibling = (1 - s, d, t)

    def far_first(n):
        return sorted(range(1, n), key=lambda k: -min(k, n - k))

    barrier = pltpu.get_barrier_semaphore()
    peers = (
        [at_x(k) for k in range(1, T)]
        + [at_y(k) for k in range(1, Y)]
        + [at_z(k) for k in range(1, Z)]
        + [sibling]
    )
    for p in peers:
        pl.semaphore_signal(barrier, inc=1, device_id=p, device_id_type=MESH)

    for c in range(3):
        W["a"][s, z, y, :, c * E : (c + 1) * E] = wq_in[c]
        pack[s, 7:8, c * E : (c + 1) * E] = bq_in[:, c * E : (c + 1) * E]
    W["a"][s, z, y, :, 3 * E :] = wo_in[...]
    W["f"][s, z, y] = wf_in[...]
    W["p"][s, z, y] = wp_in[...]
    pack[s, 0:2, :] = gains_in[...]
    pack[s, 2:6, :] = shifts_in[...]
    pack[s, 6:7, :F] = bf_in[...]
    pl.semaphore_wait(barrier, len(peers))

    pack_copy = copy(pack.at[s], pack.at[s], sibling)
    pack_copy.start()

    def on(core, f):
        pl.when(s == core)(f)

    class Gather:
        def __init__(self, l, m):
            w = W[m]
            self.l = l
            half = [pl.ds(0, HB), pl.ds(HB, HB)]

            def same(view, device, when, *key):
                return copy(view, view, device, when, ("gather", l, m) + key)

            give = w.at[l, z, y, half[1 - l]]
            self.zero = same(give, sibling, l, 0)
            zs = [(z + k) % Z for k in range(Z)]
            ys = [(y + k) % Y for k in range(Y)]
            self.one, self.two, self.far, self.over = [], [], [], []
            for h in range(2):
                own = w.at[l, z, y, half[h]]
                if h == 0:
                    n, m_, at_one, at_two, ring = Y, Z, at_y, at_z, zs

                    def strip(i, lo=0, size=Y, ring=ring, h=h):
                        return w.at[l, ring[i], pl.ds(lo, size), half[h]]

                else:
                    n, m_, at_one, at_two, ring = Z, Y, at_z, at_y, ys

                    def strip(i, lo=0, size=Z, ring=ring, h=h):
                        return w.at[l, pl.ds(lo, size), ring[i], half[h]]

                self.one.append([same(own, at_one(k), h, 1, k) for k in far_first(n)])
                self.two.append({k: same(strip(0), at_two(k), h, 2, k) for k in (1, m_ - 1)})
                self.far.append(
                    {
                        1: same(strip(m_ - 1, 0, n // 2), at_two(1), h, 3, 1),
                        m_ - 1: same(strip(1, n // 2, n // 2), at_two(m_ - 1), h, 3, 2),
                    }
                )
                if h == l:
                    first = [same(strip(0), sibling, h, 4, 0)]
                else:
                    at = [(z, (y + k) % Y) if h == 0 else ((z + k) % Z, y) for k in range(1, n)]
                    first = [
                        same(w.at[l, zz, yy, half[h]], sibling, h, 4, 0, k)
                        for k, (zz, yy) in enumerate(at)
                    ]
                self.over.append([first] + [[same(strip(i), sibling, h, 4, i)] for i in range(1, m_)])

        def s0(self):
            on(self.l, self.zero.start)

        def s1(self, h):
            if h != self.l:
                self.zero.wait_recv()
            for c in self.one[h]:
                c.start()

        def s2(self, h):
            for c in self.one[h]:
                c.wait_recv()
            for c in self.two[h].values():
                c.start()
            for c in self.over[h][0]:
                c.start()

        def s3(self, h):
            for k, c in self.two[h].items():
                c.wait_recv()
                self.far[h][k].start()
                self.over[h][1 if k != 1 else len(self.over[h]) - 1][0].start()

        def s4(self, h):
            for c in self.far[h].values():
                c.wait_recv()
            self.over[h][2][0].start()

        def s5(self, h):
            for group in self.over[1 - h]:
                for c in group:
                    c.wait_recv()

    gathers = [{m: Gather(l, m) for m in names} for l in range(2)]

    def phase(l, *steps):
        for h in range(2):

            def go(h=h):
                for one in steps:
                    getattr(gathers[l][one[0]], one[1:])(h)

            on(h, go)

    def ready(l, m):
        phase(l, m + "s5")

    for l in range(2):
        for m in names:
            gathers[l][m].s0()
    phase(0, "as1", "fs1", "ps1")

    lengths, ranks, micros = (r[...].astype(F32) for r in (len_in, rank_in, micro_in))
    n_seq = lengths.shape[1]
    mine_row = jnp.logical_and(ranks == d.astype(F32), micros == s.astype(F32))
    taken_row = jnp.where(mine_row, lengths, 0.0)
    i0 = lax.broadcasted_iota(jnp.int32, (n_seq, n_seq), 0)
    i1 = lax.broadcasted_iota(jnp.int32, (n_seq, n_seq), 1)
    taken_col = jnp.sum(jnp.where(i0 == i1, taken_row, 0.0), axis=1, keepdims=True)
    ends_col = jnp.sum(jnp.where(i1 <= i0, taken_row, 0.0), axis=1, keepdims=True)
    ends_row = jnp.sum(jnp.where(i0 <= i1, taken_col, 0.0), axis=0, keepdims=True)
    number_row = lax.broadcasted_iota(jnp.int32, (1, n_seq), 1).astype(F32) + 1.0
    number_col = lax.broadcasted_iota(jnp.int32, (n_seq, 1), 0).astype(F32) + 1.0

    def column_labels(rows, first):
        places = (lax.broadcasted_iota(jnp.int32, (rows, n_seq), 0) + first).astype(F32)
        inside = jnp.logical_and(places >= ends_row - taken_row, places < ends_row)
        return jnp.sum(jnp.where(inside, number_row, 0.0), axis=1, keepdims=True)

    label_col = column_labels(R, 0)
    places = lax.broadcasted_iota(jnp.int32, (n_seq, R), 1).astype(F32)
    inside = jnp.logical_and(places >= ends_col - taken_col, places < ends_col)
    label_row = jnp.sum(jnp.where(inside, number_col, 0.0), axis=0, keepdims=True)
    r0 = lax.broadcasted_iota(jnp.int32, (R, R), 0)
    r1 = lax.broadcasted_iota(jnp.int32, (R, R), 1)
    same = jnp.logical_and(label_col == label_row, label_col > 0.5)
    visible = jnp.logical_or(jnp.logical_and(same, r1 <= r0), r0 == r1)
    MASK[...] = jnp.where(visible, 1.0, 0.0)
    valid = [jnp.where(column_labels(HR, t * LR + h * HR) > 0.5, 1.0, 0.0) for h in range(2)]

    pack_copy.wait_recv()

    def gain(l, i):
        return pack[l, i : i + 1, :]

    def shift(l, i):
        return pack[l, 2 + i : 3 + i, :]

    halves = [slice(h * HR, h * HR + HR) for h in range(2)]
    turns = {(h, slot): [] for h in range(2) for slot in range(3)}
    turn = [0, 0]

    def next_turn(h):
        slot = turn[h] % 3
        turn[h] += 1
        for c in turns[h, slot]:
            c.wait_send()
            drains.remove(c)
        return slot

    def gather_x(buf, h):
        slot = next_turn(h)
        part = buf.at[t, pl.ds(h * HR, HR)]
        copies = [copy(part, part, at_x(k), None, ("x", slot, h, k)) for k in far_first(T)]
        for c in copies:
            c.start()
        turns[h, slot] = copies

        def wait():
            for c in copies:
                c.wait_recv()

        return wait

    scatters = [0, 0]

    def scatter_x(part, h):
        slot = next_turn(h)
        number = scatters[h]
        scatters[h] += 1
        turned = number % 2
        stage[turned, h] = part.astype(BF16).reshape(T, HR, D)
        copies = [
            copy(
                stage.at[turned, h, (t + k) % T],
                recv.at[number, h, k - 1],
                at_x(k),
                None,
                ("x", slot, h, k),
            )
            for k in far_first(T)
        ]
        for c in copies:
            c.start()
        turns[h, slot] = copies

        def total():
            for c in copies:
                c.wait_recv()
            v = stage[turned, h, t].astype(F32)
            for k in range(1, T):
                v = v + recv[number, h, k - 1].astype(F32)
            return v

        return total

    lanes = lax.broadcasted_iota(jnp.int32, (R, 2 * HD), 1)

    def half(v, h):
        keep = lanes < HD if h == 0 else lanes >= HD
        return jnp.where(keep, v, jnp.zeros_like(v))

    factor = HD ** (-0.5)

    def some(buf, l, h, lo=None, hi=None):
        v = buf[l, :, halves[h], lo:hi]
        return v.reshape(T * HR, v.shape[-1])

    def every(buf, l, lo=None, hi=None):
        v = buf[l, :, :, lo:hi]
        return v.reshape(R, v.shape[-1])

    def spread(v, n):
        return v.reshape(T, n, v.shape[-1])

    parts_of = {"q": ("a", 0, 3 * E), "o": ("a", 3 * E, 4 * E), "f": ("f", 0, F), "p": ("p", 0, F)}

    def weight(m, l):
        w, lo, hi = parts_of[m]
        return W[w][l, :, :, :, lo:hi].reshape(D, hi - lo)

    def layer_forward(l, inputs_of, at_a, at_q, at_b, at_c, at_d):
        waits = []
        for h in range(2):
            rows = halves[h]
            X = inputs_of[h]()
            n1, inv1 = norm(X)
            N1[l, rows] = n1
            I1[l, rows] = inv1
            HID[rows] = X
            A[l, t, rows] = (n1 * gain(l, 0) + shift(l, 0)).astype(BF16)
            waits.append(gather_x(A.at[l], h))
        at_a()
        ready(l, "a")
        for h in range(2):
            waits[h]()
            v = nn(some(A, l, h), weight("q", l)) + pack[l, 7:8, : 3 * E]
            QKV[l, :, halves[h], :] = spread(v.astype(BF16), HR)
        at_q()
        for pair in range(E // (2 * HD)):
            lo = pair * 2 * HD
            q2, k2, v2 = (every(QKV, l, i * E + lo, i * E + lo + 2 * HD) for i in range(3))
            o2 = None
            for h in range(2):
                S = nt(q2, half(k2, h)) * factor
                S = jnp.where(MASK[...] > 0.5, S, -1e30)
                e = jnp.exp(S - jnp.max(S, axis=-1, keepdims=True))
                pr = (e / jnp.sum(e, axis=-1, keepdims=True)).astype(BF16)
                PR[l, pair * 2 + h] = pr
                part = nn(pr, half(v2, h))
                o2 = part if o2 is None else o2 + part
            O[l, :, :, lo : lo + 2 * HD] = spread(o2.astype(BF16), LR)
        totals = [scatter_x(nt(some(O, l, h), weight("o", l)), h) for h in range(2)]
        at_b()
        waits = []
        for h in range(2):
            rows = halves[h]
            hidden = HID[rows] + totals[h]() + shift(l, 2)
            n2, inv2 = norm(hidden)
            N2[l, rows] = n2
            I2[l, rows] = inv2
            HID[rows] = hidden
            Cn[l, t, rows] = (n2 * gain(l, 1) + shift(l, 1)).astype(BF16)
            waits.append(gather_x(Cn.at[l], h))
        at_c()
        ready(l, "f")
        totals = []
        for h in range(2):
            waits[h]()
            step = F // 2
            for j in range(2):
                cols = slice(j * step, (j + 1) * step)
                u = nn(some(Cn, l, h), W["f"][l, :, :, :, cols].reshape(D, step)) + pack[l, 6:7, cols]
                U[l, :, halves[h], cols] = spread(u, HR)
                Gl[l, :, halves[h], cols] = spread(gelu(u).astype(BF16), HR)
            if h == 0:
                ready(l, "p")
            totals.append(scatter_x(nt(some(Gl, l, h), weight("p", l)), h))
        at_d()
        return [
            lambda h=h: (HID[halves[h]] + totals[h]() + shift(l, 3)) * valid[h] for h in range(2)
        ]

    def grad_matrix(m, l, left, right):
        span = D // Z
        w, lo, hi = parts_of[m]

        def step(i, carry):
            cols = pl.ds(pl.multiple_of(i * span, span), span)
            block = tn(left[:, :, cols].reshape(R, span), right())
            G[w][l, i, :, :, lo:hi] = block.astype(BF16).reshape(Y, B, hi - lo)
            return carry

        lax.fori_loop(0, Z, step, 0)

    class Reduce:
        def __init__(self, l, m):
            self.l, self.m = l, m
            g = G[m]
            half = [pl.ds(0, HB), pl.ds(HB, HB)]
            self.over = [
                copy(g.at[l, :, :, half[1 - h]], SIB[m].at[l], sibling, h, (l, m, 0)) for h in range(2)
            ]
            self.one = [
                [
                    copy(g.at[l, :, (y + k) % Y, half[0]], RA[m].at[l, k - 1], at_y(k), 0, (l, m, 1, k))
                    for k in far_first(Y)
                ],
                [
                    copy(g.at[l, (z + k) % Z, :, half[1]], RA[m].at[l, k - 1], at_z(k), 1, (l, m, 1, k))
                    for k in far_first(Z)
                ],
            ]
            self.two = [
                [
                    copy(g.at[l, (z + k) % Z, y, half[0]], R2[m].at[l, k - 1], at_z(k), 0, (l, m, 2, k))
                    for k in far_first(Z)
                ],
                [
                    copy(g.at[l, z, (y + k) % Y, half[1]], R2[m].at[l, k - 1], at_y(k), 1, (l, m, 2, k))
                    for k in far_first(Y)
                ],
            ]
            self.back = copy(FIN[m].at[0], FIN[m].at[1], sibling, 1 - l)

        def r0(self, h):
            self.over[h].start()

        def r1(self, h):
            g, l, m = G[self.m], self.l, self.m
            rows = slice(h * HB, h * HB + HB)
            self.over[1 - h].wait_recv()

            def step(i, carry):
                g[l, i, :, rows] = (g[l, i, :, rows].astype(F32) + SIB[m][l, i].astype(F32)).astype(BF16)
                return carry

            lax.fori_loop(0, Z, step, 0)
            for c in self.one[h]:
                c.start()

        def r2(self, h):
            g, l, m = G[self.m], self.l, self.m
            rows = slice(h * HB, h * HB + HB)
            for c in self.one[h]:
                c.wait_recv()
            n = len(self.one[h])
            for i in range(n + 1):
                at = (l, i, y, rows) if h == 0 else (l, z, i, rows)
                v = g[at].astype(F32)
                for k in range(n):
                    v = v + RA[m][l, k, i].astype(F32)
                g[at] = v.astype(BF16)
            for c in self.two[h]:
                c.start()

        def r3(self, h):
            g, l, m = G[self.m], self.l, self.m
            rows = slice(h * HB, h * HB + HB)
            for c in self.two[h]:
                c.wait_recv()
            v = g[l, z, y, rows].astype(F32)
            for k in range(len(self.two[h])):
                v = v + R2[m][l, k].astype(F32)
            if h == l:
                put(m, rows, v)
            else:
                FIN[m][0] = v
                self.back.start()

        def r4(self, h):
            if h == self.l:
                self.back.wait_recv()
                put(self.m, slice((1 - h) * HB, (2 - h) * HB), FIN[self.m][1])

    reduces = [{m: Reduce(l, m) for m in names} for l in range(2)]

    def task(l, *steps):
        for h in range(2):

            def go(h=h):
                for one in steps:
                    getattr(reduces[l][one[0]], one[1:])(h)

            on(h, go)

    def hand_over(l, m):
        task(l, m + "r0")

    def column_sum(v):
        return jnp.sum(v, axis=0, keepdims=True)

    def add_small(l, i, h, v):
        v = column_sum(v)
        small[l, i : i + 1, :] = v if h == 0 else small[l, i : i + 1, :] + v

    def layer_backward(l, grads_of, at_m, at_c, at_h, at_a):
        waits = []
        for h in range(2):
            dY = grads_of[h]()
            DYS[halves[h]] = dY
            DM[l, t, halves[h]] = dY.astype(BF16)
            waits.append(gather_x(DM.at[l], h))
            add_small(l, 5, h, dY)
        at_m()
        totals = []
        step = F // 2
        for h in range(2):
            waits[h]()
            for j in range(2):
                cols = slice(j * step, (j + 1) * step)
                dg = nn(some(DM, l, h), W["p"][l, :, :, :, cols].reshape(D, step))
                du = dg * gelu_slope(some(U, l, h, j * step, (j + 1) * step))
                DU[:, halves[h], cols] = spread(du.astype(BF16), HR)
            du = DU[:, halves[h], :].reshape(T * HR, F)
            totals.append(scatter_x(nt(du, weight("f", l)), h))
        grad_matrix("p", l, DM.at[l], lambda: every(Gl, l))
        hand_over(l, "p")
        grad_matrix("f", l, Cn.at[l], lambda: DU[...].reshape(R, F))
        hand_over(l, "f")
        at_c()
        waits = []
        for h in range(2):
            rows = halves[h]
            dc = totals[h]()
            dh = DYS[rows] + norm_back(dc, N2[l, rows], I2[l, rows], gain(l, 1))
            DH[l, t, rows] = dh.astype(BF16)
            waits.append(gather_x(DH.at[l], h))
            HID[rows] = dh
            add_small(l, 1, h, dc * N2[l, rows])
            add_small(l, 3, h, dc)
            add_small(l, 4, h, dh)
        small[l, 6:7, :F] = column_sum(DU[...].reshape(R, F).astype(F32))
        at_h()
        for h in range(2):
            waits[h]()
            DO[:, halves[h], :] = spread(nn(some(DH, l, h), weight("o", l)).astype(BF16), HR)
        for pair in range(E // (2 * HD)):
            lo = pair * 2 * HD
            q2, k2, v2 = (every(QKV, l, i * E + lo, i * E + lo + 2 * HD) for i in range(3))
            do2 = DO[:, :, lo : lo + 2 * HD].reshape(R, 2 * HD)
            dq = dk = dv = None
            for h in range(2):
                pr = PR[l, pair * 2 + h]
                p = pr.astype(F32)
                dp = nt(do2, half(v2, h))
                ds = (p * (dp - jnp.sum(p * dp, axis=-1, keepdims=True))).astype(BF16)
                parts = (nn(ds, half(k2, h)), tn(ds, half(q2, h)), tn(pr, half(do2, h)))
                if dq is None:
                    dq, dk, dv = parts
                else:
                    dq, dk, dv = dq + parts[0], dk + parts[1], dv + parts[2]
            for i, v in enumerate((dq * factor, dk * factor, dv)):
                DQKV[:, :, i * E + lo : i * E + lo + 2 * HD] = spread(v.astype(BF16), LR)
        totals = []
        for h in range(2):
            dqkv = DQKV[:, halves[h], :].reshape(T * HR, 3 * E)
            totals.append(scatter_x(nt(dqkv, weight("q", l)), h))
        grad_matrix("q", l, A.at[l], lambda: DQKV[...].reshape(R, 3 * E))
        grad_matrix("o", l, DH.at[l], lambda: every(O, l))
        hand_over(l, "a")
        small[l, 7:8, :] = jnp.zeros((1, D), F32)
        small[l, 7:8, : 3 * E] = column_sum(DQKV[...].reshape(R, 3 * E).astype(F32))
        at_a()

        def result(h):
            rows = halves[h]
            da = totals[h]()
            add_small(l, 0, h, da * N1[l, rows])
            add_small(l, 2, h, da)
            return HID[rows] + norm_back(da, N1[l, rows], I1[l, rows], gain(l, 0))

        return [lambda h=h: result(h) for h in range(2)]

    class Small:
        def __init__(self, l):
            self.l = l
            mine = small.at[l]
            self.over = copy(mine, small_sib, sibling, 1 - l, "small")
            self.x = [copy(mine, small_x.at[k - 1], at_x(k), l, ("small", 0, k)) for k in far_first(T)]
            self.y = [copy(small_x.at[T - 1], small_y.at[k - 1], at_y(k), l, ("small", 1, k)) for k in far_first(Y)]
            self.z = [copy(small_y.at[Y - 1], small_z.at[k - 1], at_z(k), l, ("small", 2, k)) for k in far_first(Z)]

        def begin(self):
            on(1 - self.l, self.over.start)

        def add(self):
            l = self.l
            self.over.wait_recv()
            small[l] = small[l] + small_sib[...]
            for c in self.x:
                c.start()

        def over_x(self):
            for c in self.x:
                c.wait_recv()
            v = small_x[0]
            for k in range(1, T - 1):
                v = v + small_x[k]
            row = lax.broadcasted_iota(jnp.int32, v.shape, 0)
            small_x[T - 1] = small[self.l] + jnp.where(row < 6, v, 0.0)
            for c in self.y:
                c.start()

        def over_y(self):
            for c in self.y:
                c.wait_recv()
            v = small_x[T - 1]
            for k in range(Y - 1):
                v = v + small_y[k]
            small_y[Y - 1] = v
            for c in self.z:
                c.start()

        def over_z(self):
            for c in self.z:
                c.wait_recv()
            v = small_y[Y - 1]
            for k in range(Z - 1):
                v = v + small_z[k]
            gg_out[...] = v[0:2]
            gs_out[...] = v[2:6]
            gbf_out[...] = v[6:7, :F]
            gbq_out[...] = v[7:8, : 3 * E]

    smalls = [Small(l) for l in range(2)]

    def small_task(l, step):
        on(l, getattr(smalls[l], step))

    act_copy = copy(act_send, act_recv, sibling)
    ig_copy = copy(ig_send, ig_recv, sibling)

    def f0_a():
        phase(0, "as2", "fs2", "as3", "ps2", "as4")

    def f0_q():
        phase(0, "fs3")

    def f0_b():
        phase(0, "ps3", "fs4")
        phase(1, "as1", "fs1", "ps1")

    def f0_c():
        phase(0, "ps4")
        phase(1, "as2", "fs2", "ps2")

    def f0_d():
        phase(1, "as3", "fs3")

    def f1_a():
        phase(1, "ps3", "as4")

    def f1_b():
        phase(1, "fs4", "ps4")

    def nothing():
        pass

    def keep(core, out, send, h, v):
        @pl.when(s == core)
        def _():
            out[core, halves[h]] = v

        @pl.when(s == 1 - core)
        def _():
            send[halves[h]] = v

    def sent(core, move):
        on(1 - core, move.start)

    x_of = [lambda h=h: x_in[s, halves[h]].astype(F32) for h in range(2)]
    y0 = layer_forward(0, x_of, f0_a, f0_q, f0_b, f0_c, f0_d)

    def first_output(h):
        v = y0[h]().astype(BF16)
        keep(0, act_out, act_send, h, v)
        return v.astype(F32)

    y0_of = [lambda h=h: first_output(h) for h in range(2)]

    def f1_start():
        sent(0, act_copy)
        f1_a()

    y1 = layer_forward(1, y0_of, f1_start, nothing, f1_b, nothing, nothing)

    def b1_h():
        task(1, "pr1")

    def b1_a():
        task(1, "fr1", "pr2")

    def cot_of(h):
        return cot_in[s, halves[h]].astype(F32) * valid[h]

    def b1_m():
        for h in range(2):
            keep(1, act_out, act_send, h, y1[h]().astype(BF16))
        sent(1, act_copy)

    ig1 = layer_backward(1, [lambda h=h: cot_of(h) for h in range(2)], b1_m, nothing, b1_h, b1_a)

    def ig1_of(h):
        v = ig1[h]().astype(BF16)
        keep(1, grad_out, ig_send, h, v)
        return v.astype(F32) * valid[h]

    def b0_m():
        sent(1, ig_copy)
        smalls[1].begin()
        task(1, "ar1", "fr2")
        small_task(1, "add")

    def b0_c():
        task(1, "ar2", "pr3")
        small_task(1, "over_x")

    def b0_h():
        task(1, "fr3")
        small_task(1, "over_y")
        task(0, "pr1")

    def b0_a():
        task(0, "fr1", "pr2")
        task(1, "ar3")
        small_task(1, "over_z")

    ig0 = layer_backward(0, [lambda h=h: ig1_of(h) for h in range(2)], b0_m, b0_c, b0_h, b0_a)
    task(0, "ar1", "fr2")
    for h in range(2):
        keep(0, grad_out, ig_send, h, ig0[h]().astype(BF16))
    sent(0, ig_copy)
    smalls[0].begin()

    small_task(0, "add")
    small_task(0, "over_x")
    task(0, "pr3", "ar2")
    small_task(0, "over_y")
    task(0, "fr3", "ar3")
    small_task(0, "over_z")
    for l in range(2):
        task(l, *(m + "r4" for m in names))

    act_copy.wait_recv()
    act_out[1 - s] = act_recv[...]
    ig_copy.wait_recv()
    grad_out[1 - s] = ig_recv[...]

    groups = {}
    for c in drains:
        groups.setdefault(c.when, []).append(c)
    for when, copies in groups.items():

        def drain(copies=copies):
            for c in copies:
                c.wait_send()

        if when is None:
            drain()
        else:
            on(when, drain)
    assert count[0] <= n_sems, count[0]


def split_dp(n):
    root = int(round(n**0.5))
    return n // root, root


def fused(sz, arrays, out_shape):
    names = sz.names
    Z, Y, T, LR, D, E, F, R = sz.Z, sz.Y, sz.T, sz.LR, sz.D, sz.E, sz.F, sz.R
    wd = sz.width
    n_sems = 169
    vm = pltpu.VMEM
    scratch = (
        [vm((2, Z, Y, sz.B, wd[m]), BF16) for m in names]
        + [vm((2, Z, Y, sz.B, wd[m]), BF16) for m in names]
        + [vm((2, Z, Y, sz.HB, wd[m]), BF16) for m in names]
        + [vm((2, Y - 1, Z, sz.HB, wd[m]), BF16) for m in names]
        + [vm((2, Z - 1, sz.HB, wd[m]), BF16) for m in names]
        + [vm((2, sz.HB, wd[m]), F32) for m in names]
        + [vm((2, 8, D), F32)]
        + [vm((2, T, LR, D), BF16)] * 4
        + [
            vm((2, T, LR, 3 * E), BF16),
            vm((2, T, LR, E), BF16),
            vm((2, E // HD, R, R), BF16),
            vm((2, T, LR, F), F32),
            vm((2, T, LR, F), BF16),
        ]
        + [vm((T, LR, F), BF16), vm((T, LR, E), BF16), vm((T, LR, 3 * E), BF16)]
        + [vm((2, LR, D), F32), vm((2, LR, 1), F32), vm((2, LR, D), F32), vm((2, LR, 1), F32)]
        + [vm((LR, D), F32), vm((LR, D), F32), vm((R, R), F32)]
        + [vm((2, 2, T, sz.HR, D), BF16), vm((8, 2, T - 1, sz.HR, D), BF16)]
        + [
            vm((2, 8, D), F32),
            vm((8, D), F32),
            vm((T, 8, D), F32),
            vm((Y, 8, D), F32),
            vm((Z, 8, D), F32),
        ]
        + [vm((LR, D), BF16)] * 4
        + [pltpu.SemaphoreType.DMA((n_sems,)), pltpu.SemaphoreType.DMA((n_sems,))]
    )
    spec = pl.BlockSpec(memory_space=pltpu.VMEM)

    def body(*refs):
        kernel_body(sz, n_sems, *refs)

    return pl.pallas_call(
        body,
        out_shape=out_shape,
        in_specs=[spec] * len(arrays),
        out_specs=[spec] * len(out_shape),
        scratch_shapes=scratch,
        compiler_params=pltpu.CompilerParams(
            collective_id=0, has_side_effects=True, vmem_limit_bytes=62 << 20
        ),
        name="layers",
    )(*arrays)


def hand_out(arrays):
    n = len(arrays)

    def body(*refs):
        sems = refs[2 * n]
        copies = [pltpu.make_async_copy(refs[i], refs[n + i], sems.at[i]) for i in range(n)]
        for c in copies:
            c.start()
        for c in copies:
            c.wait()

    return pl.pallas_call(
        body,
        out_shape=[jax.ShapeDtypeStruct(a.shape, a.dtype) for a in arrays],
        in_specs=[pl.BlockSpec(memory_space=pltpu.VMEM)] * n,
        out_specs=[pl.BlockSpec(memory_space=pl.ANY)] * n,
        scratch_shapes=[pltpu.SemaphoreType.DMA((n,))],
        name="hand_out",
    )(*arrays)


def per_device(*arrays):
    inputs, cotangent, w_qkv, b_qkv, w_out, w_fc, b_fc, w_proj, gains, shifts = arrays[:10]
    Z, Y = split_dp(lax.axis_size("dp"))
    T = lax.axis_size("tensor")
    E = w_qkv.shape[3]
    sz = Sizes(Z, Y, T, inputs.shape[1], inputs.shape[2], E, w_fc.shape[2])
    params = [
        w_qkv[0].transpose(1, 0, 2),
        b_qkv.reshape(1, 3 * E),
        w_out[0].T,
        w_fc[0],
        b_fc,
        w_proj[0].T,
        gains[0],
        shifts[0],
    ]
    seqs = [a.reshape(1, -1) for a in arrays[10:]]
    out_shape = [jax.ShapeDtypeStruct(inputs.shape, BF16)] * 2 + [
        jax.ShapeDtypeStruct(a.shape, F32) for a in params
    ]
    act, grad, gq, gbq, go, gf, gbf, gp, gg, gs = hand_out(
        fused(sz, [inputs, cotangent] + params + seqs, out_shape)
    )
    return (
        act[None],
        grad[None],
        gq.transpose(1, 0, 2)[None],
        gbq.reshape(1, 3, E),
        go.T[None],
        gf[None],
        gbf,
        gp.T[None],
        gg[None],
        gs[None],
    )


def solution(mesh):
    placed = (
        P(None, ("dp", "tensor"), None),
        P(None, ("dp", "tensor"), None),
        P("section", "dp", None, "tensor"),
        P("section", None, "tensor"),
        P("section", "tensor", "dp"),
        P("section", "dp", "tensor"),
        P("section", "tensor"),
        P("section", "tensor", "dp"),
        P("section", None, None),
        P("section", None, None),
        P(),
        P(),
        P(),
    )
    return jax.shard_map(
        per_device,
        mesh=mesh,
        in_specs=placed,
        out_specs=(
            P("section", None, ("dp", "tensor"), None),
            P("section", None, ("dp", "tensor"), None),
            P("section", "dp", None, "tensor"),
            P("section", None, "tensor"),
            P("section", "tensor", "dp"),
            P("section", "dp", "tensor"),
            P("section", "tensor"),
            P("section", "tensor", "dp"),
            P("section", None, None),
            P("section", None, None),
        ),
        check_vma=False,
    )
```

```python
import jax
import jax.numpy as jnp
from jax import lax
from jax.experimental import pallas as pl
from jax.experimental.pallas import tpu as pltpu
from jax.sharding import PartitionSpec as P

HD = 64
EPS = 1e-05
MESH = pl.DeviceIdType.MESH
F32 = jnp.float32
BF16 = jnp.bfloat16
GELU_A = 0.7978845608028654
GELU_B = 0.044715


def nn(a, b):
    return lax.dot_general(a, b, (((1,), (0,)), ((), ())), preferred_element_type=F32)


def nt(a, b):
    return lax.dot_general(a, b, (((1,), (1,)), ((), ())), preferred_element_type=F32)


def tn(a, b):
    return lax.dot_general(a, b, (((0,), (0,)), ((), ())), preferred_element_type=F32)


def norm(values):
    average = jnp.mean(values, axis=-1, keepdims=True)
    centered = values - average
    inv = lax.rsqrt(jnp.mean(centered * centered, axis=-1, keepdims=True) + EPS)
    return centered * inv, inv


def norm_back(grad, normal, inv, gain):
    scaled = grad * gain
    return inv * (
        scaled
        - jnp.mean(scaled, axis=-1, keepdims=True)
        - normal * jnp.mean(scaled * normal, axis=-1, keepdims=True)
    )


def gelu(u):
    return 0.5 * u * (1.0 + jnp.tanh(GELU_A * (u + GELU_B * u * u * u)))


def gelu_slope(u):
    square = u * u
    t = jnp.tanh(GELU_A * u * (1.0 + GELU_B * square))
    return 0.5 * (1.0 + t) + 0.5 * u * (1.0 - t * t) * (GELU_A * (1.0 + 3.0 * GELU_B * square))


class Sizes:
    def __init__(self, z, y, t, rows, width, heads, hidden):
        self.Z, self.Y, self.T = z, y, t
        self.LR, self.D, self.E, self.F = rows, width, heads, hidden
        self.R = rows * t
        self.HR = rows // 2
        self.B = width // (z * y)
        self.HB = self.B // 2
        self.names = ("a", "f", "p")
        self.width = {"a": 4 * heads, "f": hidden, "p": hidden}


def kernel_body(sz, n_sems, *refs):
    names = sz.names
    Z, Y, T, LR, D, E, F, R = sz.Z, sz.Y, sz.T, sz.LR, sz.D, sz.E, sz.F, sz.R
    HR, HB, B = sz.HR, sz.HB, sz.B
    it = iter(refs)
    x_in, cot_in, wq_in, bq_in, wo_in, wf_in, bf_in, wp_in, gains_in, shifts_in = (
        next(it) for _ in range(10)
    )
    len_in, rank_in, micro_in = next(it), next(it), next(it)
    act_out, grad_out, gq_out, gbq_out, go_out, gf_out, gbf_out, gp_out, gg_out, gs_out = (
        next(it) for _ in range(10)
    )

    def put(m, rows, v):
        if m == "a":
            for c in range(3):
                gq_out[c, rows, :] = v[:, c * E : (c + 1) * E]
            go_out[rows, :] = v[:, 3 * E :]
        else:
            (gf_out if m == "f" else gp_out)[rows, :] = v

    W = {m: next(it) for m in names}
    G = {m: next(it) for m in names}
    SIB = {m: next(it) for m in names}
    RA = {m: next(it) for m in names}
    R2 = {m: next(it) for m in names}
    FIN = {m: next(it) for m in names}
    pack = next(it)
    A, Cn, DM, DH = next(it), next(it), next(it), next(it)
    QKV, O, PR, U, Gl = next(it), next(it), next(it), next(it), next(it)
    DU, DO, DQKV = next(it), next(it), next(it)
    N1, I1, N2, I2 = next(it), next(it), next(it), next(it)
    HID, DYS = next(it), next(it)
    MASK = next(it)
    stage, recv = next(it), next(it)
    small, small_sib, small_x, small_y, small_z = next(it), next(it), next(it), next(it), next(it)
    act_send, act_recv, ig_send, ig_recv = next(it), next(it), next(it), next(it)
    send_sem, recv_sem = next(it), next(it)

    s = lax.axis_index("section")
    d = lax.axis_index("dp")
    t = lax.axis_index("tensor")
    z = d // Y
    y = d % Y
    count = [0]
    shared = {}
    drains = []

    class Move:
        def __init__(self, src, dst, device, when=None, key=None):
            i = shared.get(key)
            if i is None:
                i = count[0]
                count[0] += 1
                if key is not None:
                    shared[key] = i
            self.when = when
            self.made = pltpu.make_async_remote_copy(
                src_ref=src,
                dst_ref=dst,
                send_sem=send_sem.at[i],
                recv_sem=recv_sem.at[i],
                device_id=device,
                device_id_type=MESH,
            )

        def start(self):
            self.made.start()
            if self not in drains:
                drains.append(self)

        def wait_recv(self):
            self.made.wait_recv()

        def wait_send(self):
            self.made.wait_send()

    copy = Move

    def at_x(k):
        return (s, d, (t + k) % T)

    def at_y(k):
        return (s, z * Y + (y + k) % Y, t)

    def at_z(k):
        return (s, ((z + k) % Z) * Y + y, t)

    sibling = (1 - s, d, t)

    def far_first(n):
        return sorted(range(1, n), key=lambda k: -min(k, n - k))

    barrier = pltpu.get_barrier_semaphore()
    peers = (
        [at_x(k) for k in range(1, T)]
        + [at_y(k) for k in range(1, Y)]
        + [at_z(k) for k in range(1, Z)]
        + [(1 - s, d, (t + k) % T) for k in range(T)]
    )
    for p in peers:
        pl.semaphore_signal(barrier, inc=1, device_id=p, device_id_type=MESH)

    for c in range(3):
        W["a"][s, z, y, :, c * E : (c + 1) * E] = wq_in[c]
        pack[s, 7:8, c * E : (c + 1) * E] = bq_in[:, c * E : (c + 1) * E]
    W["a"][s, z, y, :, 3 * E :] = wo_in[...]
    W["f"][s, z, y] = wf_in[...]
    W["p"][s, z, y] = wp_in[...]
    pack[s, 0:2, :] = gains_in[...]
    pack[s, 2:6, :] = shifts_in[...]
    pack[s, 6:7, :F] = bf_in[...]
    pl.semaphore_wait(barrier, len(peers))

    pack_copy = copy(pack.at[s], pack.at[s], sibling)
    pack_copy.start()

    def on(core, f):
        pl.when(s == core)(f)

    class Gather:
        def __init__(self, l, m):
            w = W[m]
            self.l = l
            half = [pl.ds(0, HB), pl.ds(HB, HB)]

            def same(view, device, when, *key):
                return copy(view, view, device, when, ("gather", l, m) + key)

            give = w.at[l, z, y, half[1 - l]]
            self.zero = same(give, sibling, l, 0)
            zs = [(z + k) % Z for k in range(Z)]
            ys = [(y + k) % Y for k in range(Y)]
            self.one, self.two, self.far, self.over = [], [], [], []
            for h in range(2):
                own = w.at[l, z, y, half[h]]
                if h == 0:
                    n, m_, at_one, at_two, ring = Y, Z, at_y, at_z, zs

                    def strip(i, lo=0, size=Y, ring=ring, h=h):
                        return w.at[l, ring[i], pl.ds(lo, size), half[h]]

                else:
                    n, m_, at_one, at_two, ring = Z, Y, at_z, at_y, ys

                    def strip(i, lo=0, size=Z, ring=ring, h=h):
                        return w.at[l, pl.ds(lo, size), ring[i], half[h]]

                self.one.append([same(own, at_one(k), h, 1, k) for k in far_first(n)])
                self.two.append({k: same(strip(0), at_two(k), h, 2, k) for k in (1, m_ - 1)})
                self.far.append(
                    {
                        1: same(strip(m_ - 1, 0, n // 2), at_two(1), h, 3, 1),
                        m_ - 1: same(strip(1, n // 2, n // 2), at_two(m_ - 1), h, 3, 2),
                    }
                )
                if h == l:
                    first = [same(strip(0), sibling, h, 4, 0)]
                else:
                    at = [(z, (y + k) % Y) if h == 0 else ((z + k) % Z, y) for k in range(1, n)]
                    first = [
                        same(w.at[l, zz, yy, half[h]], sibling, h, 4, 0, k)
                        for k, (zz, yy) in enumerate(at)
                    ]
                self.over.append([first] + [[same(strip(i), sibling, h, 4, i)] for i in range(1, m_)])

        def s0(self):
            on(self.l, self.zero.start)

        def s1(self, h):
            if h != self.l:
                self.zero.wait_recv()
            for c in self.one[h]:
                c.start()

        def s2(self, h):
            for c in self.one[h]:
                c.wait_recv()
            for c in self.two[h].values():
                c.start()
            for c in self.over[h][0]:
                c.start()

        def s3(self, h):
            for k, c in self.two[h].items():
                c.wait_recv()
                self.far[h][k].start()
                self.over[h][1 if k != 1 else len(self.over[h]) - 1][0].start()

        def s4(self, h):
            for c in self.far[h].values():
                c.wait_recv()
            self.over[h][2][0].start()

        def s5(self, h):
            for group in self.over[1 - h]:
                for c in group:
                    c.wait_recv()

    gathers = [{m: Gather(l, m) for m in names} for l in range(2)]

    def phase(l, *steps):
        for h in range(2):

            def go(h=h):
                for one in steps:
                    getattr(gathers[l][one[0]], one[1:])(h)

            on(h, go)

    def ready(l, m):
        phase(l, m + "s5")

    for l in range(2):
        for m in names:
            gathers[l][m].s0()
    phase(0, "as1", "fs1", "ps1")

    lengths, ranks, micros = (r[...].astype(F32) for r in (len_in, rank_in, micro_in))
    n_seq = lengths.shape[1]
    mine_row = jnp.logical_and(ranks == d.astype(F32), micros == s.astype(F32))
    taken_row = jnp.where(mine_row, lengths, 0.0)
    i0 = lax.broadcasted_iota(jnp.int32, (n_seq, n_seq), 0)
    i1 = lax.broadcasted_iota(jnp.int32, (n_seq, n_seq), 1)
    taken_col = jnp.sum(jnp.where(i0 == i1, taken_row, 0.0), axis=1, keepdims=True)
    ends_col = jnp.sum(jnp.where(i1 <= i0, taken_row, 0.0), axis=1, keepdims=True)
    ends_row = jnp.sum(jnp.where(i0 <= i1, taken_col, 0.0), axis=0, keepdims=True)
    number_row = lax.broadcasted_iota(jnp.int32, (1, n_seq), 1).astype(F32) + 1.0
    number_col = lax.broadcasted_iota(jnp.int32, (n_seq, 1), 0).astype(F32) + 1.0

    def column_labels(rows, first):
        places = (lax.broadcasted_iota(jnp.int32, (rows, n_seq), 0) + first).astype(F32)
        inside = jnp.logical_and(places >= ends_row - taken_row, places < ends_row)
        return jnp.sum(jnp.where(inside, number_row, 0.0), axis=1, keepdims=True)

    label_col = column_labels(R, 0)
    places = lax.broadcasted_iota(jnp.int32, (n_seq, R), 1).astype(F32)
    inside = jnp.logical_and(places >= ends_col - taken_col, places < ends_col)
    label_row = jnp.sum(jnp.where(inside, number_col, 0.0), axis=0, keepdims=True)
    r0 = lax.broadcasted_iota(jnp.int32, (R, R), 0)
    r1 = lax.broadcasted_iota(jnp.int32, (R, R), 1)
    same = jnp.logical_and(label_col == label_row, label_col > 0.5)
    visible = jnp.logical_or(jnp.logical_and(same, r1 <= r0), r0 == r1)
    MASK[...] = jnp.where(visible, 1.0, 0.0)
    valid = [jnp.where(column_labels(HR, t * LR + h * HR) > 0.5, 1.0, 0.0) for h in range(2)]

    pack_copy.wait_recv()

    def gain(l, i):
        return pack[l, i : i + 1, :]

    def shift(l, i):
        return pack[l, 2 + i : 3 + i, :]

    halves = [slice(h * HR, h * HR + HR) for h in range(2)]
    turns = {(h, slot): [] for h in range(2) for slot in range(3)}
    turn = [0, 0]

    def next_turn(h):
        slot = turn[h] % 3
        turn[h] += 1
        for c in turns[h, slot]:
            c.wait_send()
            drains.remove(c)
        return slot

    def gather_x(buf, h):
        slot = next_turn(h)
        part = buf.at[t, pl.ds(h * HR, HR)]
        copies = [copy(part, part, at_x(k), None, ("x", slot, h, k)) for k in far_first(T)]
        for c in copies:
            c.start()
        turns[h, slot] = copies

        def wait():
            for c in copies:
                c.wait_recv()

        return wait

    scatters = [0, 0]

    def scatter_x(part, h):
        slot = next_turn(h)
        number = scatters[h]
        scatters[h] += 1
        turned = number % 2
        stage[turned, h] = part.astype(BF16).reshape(T, HR, D)
        copies = [
            copy(
                stage.at[turned, h, (t + k) % T],
                recv.at[number, h, k - 1],
                at_x(k),
                None,
                ("x", slot, h, k),
            )
            for k in far_first(T)
        ]
        for c in copies:
            c.start()
        turns[h, slot] = copies

        def total():
            for c in copies:
                c.wait_recv()
            v = stage[turned, h, t].astype(F32)
            for k in range(1, T):
                v = v + recv[number, h, k - 1].astype(F32)
            return v

        return total

    lanes = lax.broadcasted_iota(jnp.int32, (R, 2 * HD), 1)

    def half(v, h):
        keep = lanes < HD if h == 0 else lanes >= HD
        return jnp.where(keep, v, jnp.zeros_like(v))

    factor = HD ** (-0.5)

    def some(buf, l, h, lo=None, hi=None):
        v = buf[l, :, halves[h], lo:hi]
        return v.reshape(T * HR, v.shape[-1])

    def every(buf, l, lo=None, hi=None):
        v = buf[l, :, :, lo:hi]
        return v.reshape(R, v.shape[-1])

    def spread(v, n):
        return v.reshape(T, n, v.shape[-1])

    parts_of = {"q": ("a", 0, 3 * E), "o": ("a", 3 * E, 4 * E), "f": ("f", 0, F), "p": ("p", 0, F)}

    def weight(m, l):
        w, lo, hi = parts_of[m]
        return W[w][l, :, :, :, lo:hi].reshape(D, hi - lo)

    def layer_forward(l, inputs_of, at_a, at_q, at_b, at_c, at_d):
        waits = []
        for h in range(2):
            rows = halves[h]
            X = inputs_of[h]()
            n1, inv1 = norm(X)
            N1[l, rows] = n1
            I1[l, rows] = inv1
            HID[rows] = X
            A[l, t, rows] = (n1 * gain(l, 0) + shift(l, 0)).astype(BF16)
            waits.append(gather_x(A.at[l], h))
        at_a()
        ready(l, "a")
        for h in range(2):
            waits[h]()
            v = nn(some(A, l, h), weight("q", l)) + pack[l, 7:8, : 3 * E]
            QKV[l, :, halves[h], :] = spread(v.astype(BF16), HR)
        at_q()
        for pair in range(E // (2 * HD)):
            lo = pair * 2 * HD
            q2, k2, v2 = (every(QKV, l, i * E + lo, i * E + lo + 2 * HD) for i in range(3))
            o2 = None
            for h in range(2):
                S = nt(q2, half(k2, h)) * factor
                S = jnp.where(MASK[...] > 0.5, S, -1e30)
                e = jnp.exp(S - jnp.max(S, axis=-1, keepdims=True))
                pr = (e / jnp.sum(e, axis=-1, keepdims=True)).astype(BF16)
                PR[l, pair * 2 + h] = pr
                part = nn(pr, half(v2, h))
                o2 = part if o2 is None else o2 + part
            O[l, :, :, lo : lo + 2 * HD] = spread(o2.astype(BF16), LR)
        totals = [scatter_x(nt(some(O, l, h), weight("o", l)), h) for h in range(2)]
        at_b()
        waits = []
        for h in range(2):
            rows = halves[h]
            hidden = HID[rows] + totals[h]() + shift(l, 2)
            n2, inv2 = norm(hidden)
            N2[l, rows] = n2
            I2[l, rows] = inv2
            HID[rows] = hidden
            Cn[l, t, rows] = (n2 * gain(l, 1) + shift(l, 1)).astype(BF16)
            waits.append(gather_x(Cn.at[l], h))
        at_c()
        ready(l, "f")
        totals = []
        for h in range(2):
            waits[h]()
            step = F // 2
            for j in range(2):
                cols = slice(j * step, (j + 1) * step)
                u = nn(some(Cn, l, h), W["f"][l, :, :, :, cols].reshape(D, step)) + pack[l, 6:7, cols]
                U[l, :, halves[h], cols] = spread(u, HR)
                Gl[l, :, halves[h], cols] = spread(gelu(u).astype(BF16), HR)
            if h == 0:
                ready(l, "p")
            totals.append(scatter_x(nt(some(Gl, l, h), weight("p", l)), h))
        at_d()
        return [
            lambda h=h: (HID[halves[h]] + totals[h]() + shift(l, 3)) * valid[h] for h in range(2)
        ]

    def grad_matrix(m, l, left, right):
        span = D // Z
        w, lo, hi = parts_of[m]

        def step(i, carry):
            cols = pl.ds(pl.multiple_of(i * span, span), span)
            block = tn(left[:, :, cols].reshape(R, span), right())
            G[w][l, i, :, :, lo:hi] = block.astype(BF16).reshape(Y, B, hi - lo)
            return carry

        lax.fori_loop(0, Z, step, 0)

    class Reduce:
        def __init__(self, l, m):
            self.l, self.m = l, m
            g = G[m]
            half = [pl.ds(0, HB), pl.ds(HB, HB)]
            self.over = [
                copy(g.at[l, :, :, half[1 - h]], SIB[m].at[l], sibling, h, (l, m, 0)) for h in range(2)
            ]
            self.one = [
                [
                    copy(g.at[l, :, (y + k) % Y, half[0]], RA[m].at[l, k - 1], at_y(k), 0, (l, m, 1, k))
                    for k in far_first(Y)
                ],
                [
                    copy(g.at[l, (z + k) % Z, :, half[1]], RA[m].at[l, k - 1], at_z(k), 1, (l, m, 1, k))
                    for k in far_first(Z)
                ],
            ]
            self.two = [
                [
                    copy(g.at[l, (z + k) % Z, y, half[0]], R2[m].at[l, k - 1], at_z(k), 0, (l, m, 2, k))
                    for k in far_first(Z)
                ],
                [
                    copy(g.at[l, z, (y + k) % Y, half[1]], R2[m].at[l, k - 1], at_y(k), 1, (l, m, 2, k))
                    for k in far_first(Y)
                ],
            ]
            self.back = copy(FIN[m].at[0], FIN[m].at[1], sibling, 1 - l)

        def r0(self, h):
            self.over[h].start()

        def r1(self, h):
            g, l, m = G[self.m], self.l, self.m
            rows = slice(h * HB, h * HB + HB)
            self.over[1 - h].wait_recv()

            def step(i, carry):
                g[l, i, :, rows] = (g[l, i, :, rows].astype(F32) + SIB[m][l, i].astype(F32)).astype(BF16)
                return carry

            lax.fori_loop(0, Z, step, 0)
            for c in self.one[h]:
                c.start()

        def r2(self, h):
            g, l, m = G[self.m], self.l, self.m
            rows = slice(h * HB, h * HB + HB)
            for c in self.one[h]:
                c.wait_recv()
            n = len(self.one[h])
            for i in range(n + 1):
                at = (l, i, y, rows) if h == 0 else (l, z, i, rows)
                v = g[at].astype(F32)
                for k in range(n):
                    v = v + RA[m][l, k, i].astype(F32)
                g[at] = v.astype(BF16)
            for c in self.two[h]:
                c.start()

        def r3(self, h):
            g, l, m = G[self.m], self.l, self.m
            rows = slice(h * HB, h * HB + HB)
            for c in self.two[h]:
                c.wait_recv()
            v = g[l, z, y, rows].astype(F32)
            for k in range(len(self.two[h])):
                v = v + R2[m][l, k].astype(F32)
            if h == l:
                put(m, rows, v)
            else:
                FIN[m][0] = v
                self.back.start()

        def r4(self, h):
            if h == self.l:
                self.back.wait_recv()
                put(self.m, slice((1 - h) * HB, (2 - h) * HB), FIN[self.m][1])

    reduces = [{m: Reduce(l, m) for m in names} for l in range(2)]

    def task(l, *steps):
        for h in range(2):

            def go(h=h):
                for one in steps:
                    getattr(reduces[l][one[0]], one[1:])(h)

            on(h, go)

    def hand_over(l, m):
        task(l, m + "r0")

    def column_sum(v):
        return jnp.sum(v, axis=0, keepdims=True)

    def add_small(l, i, h, v):
        v = column_sum(v)
        small[l, i : i + 1, :] = v if h == 0 else small[l, i : i + 1, :] + v

    def layer_backward(l, grads_of, at_m, at_c, at_h, at_a):
        waits = []
        for h in range(2):
            dY = grads_of[h]()
            DYS[halves[h]] = dY
            DM[l, t, halves[h]] = dY.astype(BF16)
            waits.append(gather_x(DM.at[l], h))
            add_small(l, 5, h, dY)
        at_m()
        totals = []
        step = F // 2
        for h in range(2):
            waits[h]()
            for j in range(2):
                cols = slice(j * step, (j + 1) * step)
                dg = nn(some(DM, l, h), W["p"][l, :, :, :, cols].reshape(D, step))
                du = dg * gelu_slope(some(U, l, h, j * step, (j + 1) * step))
                DU[:, halves[h], cols] = spread(du.astype(BF16), HR)
            du = DU[:, halves[h], :].reshape(T * HR, F)
            totals.append(scatter_x(nt(du, weight("f", l)), h))
        grad_matrix("p", l, DM.at[l], lambda: every(Gl, l))
        hand_over(l, "p")
        grad_matrix("f", l, Cn.at[l], lambda: DU[...].reshape(R, F))
        hand_over(l, "f")
        at_c()
        waits = []
        for h in range(2):
            rows = halves[h]
            dc = totals[h]()
            dh = DYS[rows] + norm_back(dc, N2[l, rows], I2[l, rows], gain(l, 1))
            DH[l, t, rows] = dh.astype(BF16)
            waits.append(gather_x(DH.at[l], h))
            HID[rows] = dh
            add_small(l, 1, h, dc * N2[l, rows])
            add_small(l, 3, h, dc)
            add_small(l, 4, h, dh)
        small[l, 6:7, :F] = column_sum(DU[...].reshape(R, F).astype(F32))
        at_h()
        for h in range(2):
            waits[h]()
            DO[:, halves[h], :] = spread(nn(some(DH, l, h), weight("o", l)).astype(BF16), HR)
        if l == 0:
            grad_matrix("o", l, DH.at[l], lambda: every(O, l))
        for pair in range(E // (2 * HD)):
            lo = pair * 2 * HD
            q2, k2, v2 = (every(QKV, l, i * E + lo, i * E + lo + 2 * HD) for i in range(3))
            do2 = DO[:, :, lo : lo + 2 * HD].reshape(R, 2 * HD)
            dq = dk = dv = None
            for h in range(2):
                pr = PR[l, pair * 2 + h]
                p = pr.astype(F32)
                dp = nt(do2, half(v2, h))
                ds = (p * (dp - jnp.sum(p * dp, axis=-1, keepdims=True))).astype(BF16)
                parts = (nn(ds, half(k2, h)), tn(ds, half(q2, h)), tn(pr, half(do2, h)))
                if dq is None:
                    dq, dk, dv = parts
                else:
                    dq, dk, dv = dq + parts[0], dk + parts[1], dv + parts[2]
            for i, v in enumerate((dq * factor, dk * factor, dv)):
                DQKV[:, :, i * E + lo : i * E + lo + 2 * HD] = spread(v.astype(BF16), LR)
        totals = []
        for h in range(2):
            dqkv = DQKV[:, halves[h], :].reshape(T * HR, 3 * E)
            totals.append(scatter_x(nt(dqkv, weight("q", l)), h))
        grad_matrix("q", l, A.at[l], lambda: DQKV[...].reshape(R, 3 * E))
        if l == 1:
            grad_matrix("o", l, DH.at[l], lambda: every(O, l))
        hand_over(l, "a")
        small[l, 7:8, :] = jnp.zeros((1, D), F32)
        small[l, 7:8, : 3 * E] = column_sum(DQKV[...].reshape(R, 3 * E).astype(F32))
        at_a()

        def result(h):
            rows = halves[h]
            da = totals[h]()
            add_small(l, 0, h, da * N1[l, rows])
            add_small(l, 2, h, da)
            return HID[rows] + norm_back(da, N1[l, rows], I1[l, rows], gain(l, 0))

        return [lambda h=h: result(h) for h in range(2)]

    class Small:
        def __init__(self, l):
            self.l = l
            mine = small.at[l]
            self.over = [
                copy(mine, small_sib.at[k], (1 - s, d, (t + k) % T), 1 - l, ("small", 3, k))
                for k in far_first(T) + [0]
            ]
            self.x = [
                copy(mine, small_x.at[k - 1], at_x(k), l, ("small", 0, k)) for k in far_first(T)
            ]
            self.y = [copy(small_x.at[T - 1], small_y.at[k - 1], at_y(k), l, ("small", 1, k)) for k in far_first(Y)]
            self.z = [copy(small_y.at[Y - 1], small_z.at[k - 1], at_z(k), l, ("small", 2, k)) for k in far_first(Z)]

        def begin(self):
            def go(copies):
                for c in copies:
                    c.start()

            on(1 - self.l, lambda: go(self.over))
            on(self.l, lambda: go(self.x))

        def over_x(self):
            for c in self.x + self.over:
                c.wait_recv()
            v = small_x[0] + small_sib[1]
            for k in range(1, T - 1):
                v = v + small_x[k] + small_sib[k + 1]
            row = lax.broadcasted_iota(jnp.int32, v.shape, 0)
            small_x[T - 1] = small[self.l] + small_sib[0] + jnp.where(row < 6, v, 0.0)
            for c in self.y:
                c.start()

        def over_y(self):
            for c in self.y:
                c.wait_recv()
            v = small_x[T - 1]
            for k in range(Y - 1):
                v = v + small_y[k]
            small_y[Y - 1] = v
            for c in self.z:
                c.start()

        def over_z(self):
            for c in self.z:
                c.wait_recv()
            v = small_y[Y - 1]
            for k in range(Z - 1):
                v = v + small_z[k]
            gg_out[...] = v[0:2]
            gs_out[...] = v[2:6]
            gbf_out[...] = v[6:7, :F]
            gbq_out[...] = v[7:8, : 3 * E]

    smalls = [Small(l) for l in range(2)]

    def small_task(l, step):
        on(l, getattr(smalls[l], step))

    act_copy = copy(act_send, act_recv, sibling)
    ig_copy = copy(ig_send, ig_recv, sibling)

    def f0_a():
        phase(0, "as2", "fs2", "as3", "ps2", "as4")

    def f0_q():
        phase(0, "fs3")

    def f0_b():
        phase(0, "ps3", "fs4")
        phase(1, "as1", "fs1", "ps1")

    def f0_c():
        phase(0, "ps4")
        phase(1, "as2", "fs2", "ps2")

    def f0_d():
        phase(1, "as3", "fs3")

    def f1_a():
        phase(1, "ps3", "as4")

    def f1_b():
        phase(1, "fs4", "ps4")

    def nothing():
        pass

    def keep(core, out, send, h, v):
        @pl.when(s == core)
        def _():
            out[core, halves[h]] = v

        @pl.when(s == 1 - core)
        def _():
            send[halves[h]] = v

    def sent(core, move):
        on(1 - core, move.start)

    x_of = [lambda h=h: x_in[s, halves[h]].astype(F32) for h in range(2)]
    y0 = layer_forward(0, x_of, f0_a, f0_q, f0_b, f0_c, f0_d)

    def first_output(h):
        v = y0[h]().astype(BF16)
        keep(0, act_out, act_send, h, v)
        return v.astype(F32)

    y0_of = [lambda h=h: first_output(h) for h in range(2)]

    def f1_start():
        sent(0, act_copy)
        f1_a()

    y1 = layer_forward(1, y0_of, f1_start, nothing, f1_b, nothing, nothing)

    def b1_h():
        task(1, "pr1", "fr1")

    def b1_a():
        task(1, "pr2")

    def cot_of(h):
        return cot_in[s, halves[h]].astype(F32) * valid[h]

    def b1_m():
        for h in range(2):
            keep(1, act_out, act_send, h, y1[h]().astype(BF16))
        sent(1, act_copy)

    ig1 = layer_backward(1, [lambda h=h: cot_of(h) for h in range(2)], b1_m, nothing, b1_h, b1_a)

    def ig1_of(h):
        v = ig1[h]().astype(BF16)
        keep(1, grad_out, ig_send, h, v)
        return v.astype(F32) * valid[h]

    def b0_m():
        sent(1, ig_copy)
        smalls[1].begin()
        task(1, "ar1", "fr2")

    def b0_c():
        task(1, "ar2", "pr3")
        small_task(1, "over_x")

    def b0_h():
        task(0, "pr1", "fr1")
        task(1, "fr3")
        small_task(1, "over_y")

    def b0_a():
        task(0, "ar1", "pr2", "fr2")
        task(1, "ar3")
        small_task(1, "over_z")

    ig0 = layer_backward(0, [lambda h=h: ig1_of(h) for h in range(2)], b0_m, b0_c, b0_h, b0_a)
    for h in range(2):
        keep(0, grad_out, ig_send, h, ig0[h]().astype(BF16))
    sent(0, ig_copy)
    smalls[0].begin()

    task(0, "pr3", "fr3")
    small_task(0, "over_x")
    task(0, "ar2")
    small_task(0, "over_y")
    for l, m in ((1, "a"), (1, "f"), (1, "p"), (0, "p"), (0, "f")):
        task(l, m + "r4")
    task(0, "ar3")
    small_task(0, "over_z")
    task(0, "ar4")

    act_copy.wait_recv()
    act_out[1 - s] = act_recv[...]
    ig_copy.wait_recv()
    grad_out[1 - s] = ig_recv[...]

    groups = {}
    for c in drains:
        groups.setdefault(c.when, []).append(c)
    for when, copies in groups.items():

        def drain(copies=copies):
            for c in copies:
                c.wait_send()

        if when is None:
            drain()
        else:
            on(when, drain)
    assert count[0] <= n_sems, count[0]


def split_dp(n):
    root = int(round(n**0.5))
    return n // root, root


def fused(sz, arrays, out_shape):
    names = sz.names
    Z, Y, T, LR, D, E, F, R = sz.Z, sz.Y, sz.T, sz.LR, sz.D, sz.E, sz.F, sz.R
    wd = sz.width
    n_sems = 172
    vm = pltpu.VMEM
    scratch = (
        [vm((2, Z, Y, sz.B, wd[m]), BF16) for m in names]
        + [vm((2, Z, Y, sz.B, wd[m]), BF16) for m in names]
        + [vm((2, Z, Y, sz.HB, wd[m]), BF16) for m in names]
        + [vm((2, Y - 1, Z, sz.HB, wd[m]), BF16) for m in names]
        + [vm((2, Z - 1, sz.HB, wd[m]), BF16) for m in names]
        + [vm((2, sz.HB, wd[m]), F32) for m in names]
        + [vm((2, 8, D), F32)]
        + [vm((2, T, LR, D), BF16)] * 4
        + [
            vm((2, T, LR, 3 * E), BF16),
            vm((2, T, LR, E), BF16),
            vm((2, E // HD, R, R), BF16),
            vm((2, T, LR, F), F32),
            vm((2, T, LR, F), BF16),
        ]
        + [vm((T, LR, F), BF16), vm((T, LR, E), BF16), vm((T, LR, 3 * E), BF16)]
        + [vm((2, LR, D), F32), vm((2, LR, 1), F32), vm((2, LR, D), F32), vm((2, LR, 1), F32)]
        + [vm((LR, D), F32), vm((LR, D), F32), vm((R, R), F32)]
        + [vm((2, 2, T, sz.HR, D), BF16), vm((8, 2, T - 1, sz.HR, D), BF16)]
        + [
            vm((2, 8, D), F32),
            vm((T, 8, D), F32),
            vm((T, 8, D), F32),
            vm((Y, 8, D), F32),
            vm((Z, 8, D), F32),
        ]
        + [vm((LR, D), BF16)] * 4
        + [pltpu.SemaphoreType.DMA((n_sems,)), pltpu.SemaphoreType.DMA((n_sems,))]
    )
    spec = pl.BlockSpec(memory_space=pltpu.VMEM)

    def body(*refs):
        kernel_body(sz, n_sems, *refs)

    return pl.pallas_call(
        body,
        out_shape=out_shape,
        in_specs=[spec] * len(arrays),
        out_specs=[spec] * len(out_shape),
        scratch_shapes=scratch,
        compiler_params=pltpu.CompilerParams(
            collective_id=0, has_side_effects=True, vmem_limit_bytes=62 << 20
        ),
        name="layers",
    )(*arrays)


def hand_out(arrays):
    n = len(arrays)

    def body(*refs):
        sems = refs[2 * n]
        copies = [pltpu.make_async_copy(refs[i], refs[n + i], sems.at[i]) for i in range(n)]
        for c in copies:
            c.start()
        for c in copies:
            c.wait()

    return pl.pallas_call(
        body,
        out_shape=[jax.ShapeDtypeStruct(a.shape, a.dtype) for a in arrays],
        in_specs=[pl.BlockSpec(memory_space=pltpu.VMEM)] * n,
        out_specs=[pl.BlockSpec(memory_space=pl.ANY)] * n,
        scratch_shapes=[pltpu.SemaphoreType.DMA((n,))],
        name="hand_out",
    )(*arrays)


def per_device(*arrays):
    inputs, cotangent, w_qkv, b_qkv, w_out, w_fc, b_fc, w_proj, gains, shifts = arrays[:10]
    Z, Y = split_dp(lax.axis_size("dp"))
    T = lax.axis_size("tensor")
    E = w_qkv.shape[3]
    sz = Sizes(Z, Y, T, inputs.shape[1], inputs.shape[2], E, w_fc.shape[2])
    params = [
        w_qkv[0].transpose(1, 0, 2),
        b_qkv.reshape(1, 3 * E),
        w_out[0].T,
        w_fc[0],
        b_fc,
        w_proj[0].T,
        gains[0],
        shifts[0],
    ]
    seqs = [a.reshape(1, -1) for a in arrays[10:]]
    out_shape = [jax.ShapeDtypeStruct(inputs.shape, BF16)] * 2 + [
        jax.ShapeDtypeStruct(a.shape, F32) for a in params
    ]
    act, grad, gq, gbq, go, gf, gbf, gp, gg, gs = hand_out(
        fused(sz, [inputs, cotangent] + params + seqs, out_shape)
    )
    return (
        act[None],
        grad[None],
        gq.transpose(1, 0, 2)[None],
        gbq.reshape(1, 3, E),
        go.T[None],
        gf[None],
        gbf,
        gp.T[None],
        gg[None],
        gs[None],
    )


def solution(mesh):
    placed = (
        P(None, ("dp", "tensor"), None),
        P(None, ("dp", "tensor"), None),
        P("section", "dp", None, "tensor"),
        P("section", None, "tensor"),
        P("section", "tensor", "dp"),
        P("section", "dp", "tensor"),
        P("section", "tensor"),
        P("section", "tensor", "dp"),
        P("section", None, None),
        P("section", None, None),
        P(),
        P(),
        P(),
    )
    return jax.shard_map(
        per_device,
        mesh=mesh,
        in_specs=placed,
        out_specs=(
            P("section", None, ("dp", "tensor"), None),
            P("section", None, ("dp", "tensor"), None),
            P("section", "dp", None, "tensor"),
            P("section", None, "tensor"),
            P("section", "tensor", "dp"),
            P("section", "dp", "tensor"),
            P("section", "tensor"),
            P("section", "tensor", "dp"),
            P("section", None, None),
            P("section", None, None),
        ),
        check_vma=False,
    )
```

```python
import jax
import jax.numpy as jnp
from jax import lax
from jax.experimental import pallas as pl
from jax.experimental.pallas import tpu as pltpu
from jax.sharding import PartitionSpec as P

HD = 64
EPS = 1e-05
MESH = pl.DeviceIdType.MESH
F32 = jnp.float32
BF16 = jnp.bfloat16
GELU_A = 0.7978845608028654
GELU_B = 0.044715


def nn(a, b):
    return lax.dot_general(a, b, (((1,), (0,)), ((), ())), preferred_element_type=F32)


def nt(a, b):
    return lax.dot_general(a, b, (((1,), (1,)), ((), ())), preferred_element_type=F32)


def tn(a, b):
    return lax.dot_general(a, b, (((0,), (0,)), ((), ())), preferred_element_type=F32)


def norm(values):
    average = jnp.mean(values, axis=-1, keepdims=True)
    centered = values - average
    inv = lax.rsqrt(jnp.mean(centered * centered, axis=-1, keepdims=True) + EPS)
    return centered * inv, inv


def norm_back(grad, normal, inv, gain):
    scaled = grad * gain
    return inv * (
        scaled
        - jnp.mean(scaled, axis=-1, keepdims=True)
        - normal * jnp.mean(scaled * normal, axis=-1, keepdims=True)
    )


def gelu(u):
    return 0.5 * u * (1.0 + jnp.tanh(GELU_A * (u + GELU_B * u * u * u)))


def gelu_slope(u):
    square = u * u
    t = jnp.tanh(GELU_A * u * (1.0 + GELU_B * square))
    return 0.5 * (1.0 + t) + 0.5 * u * (1.0 - t * t) * (GELU_A * (1.0 + 3.0 * GELU_B * square))


class Sizes:
    def __init__(self, z, y, t, rows, width, heads, hidden):
        self.Z, self.Y, self.T = z, y, t
        self.LR, self.D, self.E, self.F = rows, width, heads, hidden
        self.R = rows * t
        self.HR = rows // 2
        self.B = width // (z * y)
        self.HB = self.B // 2
        self.names = ("a", "f", "p")
        self.width = {"a": 4 * heads, "f": hidden, "p": hidden}


def kernel_body(sz, n_sems, *refs):
    names = sz.names
    Z, Y, T, LR, D, E, F, R = sz.Z, sz.Y, sz.T, sz.LR, sz.D, sz.E, sz.F, sz.R
    HR, HB, B = sz.HR, sz.HB, sz.B
    it = iter(refs)
    x_in, cot_in, wq_in, bq_in, wo_in, wf_in, bf_in, wp_in, gains_in, shifts_in = (
        next(it) for _ in range(10)
    )
    len_in, rank_in, micro_in = next(it), next(it), next(it)
    act_out, grad_out, gq_out, gbq_out, go_out, gf_out, gbf_out, gp_out, gg_out, gs_out = (
        next(it) for _ in range(10)
    )

    def put(m, rows, v):
        if m == "a":
            for c in range(3):
                gq_out[c, rows, :] = v[:, c * E : (c + 1) * E]
            go_out[rows, :] = v[:, 3 * E :]
        else:
            (gf_out if m == "f" else gp_out)[rows, :] = v

    W = {m: next(it) for m in names}
    G = {m: next(it) for m in names}
    SIB = {m: next(it) for m in names}
    RA = {m: next(it) for m in names}
    R2 = {m: next(it) for m in names}
    FIN = {m: next(it) for m in names}
    pack = next(it)
    A, Cn, DM, DH = next(it), next(it), next(it), next(it)
    QKV, O, PR, U, Gl = next(it), next(it), next(it), next(it), next(it)
    DU, DO, DQKV = next(it), next(it), next(it)
    N1, I1, N2, I2 = next(it), next(it), next(it), next(it)
    HID, DYS = next(it), next(it)
    MASK = next(it)
    stage, recv = next(it), next(it)
    small, small_sib, small_x, small_y, small_z = next(it), next(it), next(it), next(it), next(it)
    act_send, act_recv, ig_send, ig_recv = next(it), next(it), next(it), next(it)
    send_sem, recv_sem = next(it), next(it)

    s = lax.axis_index("section")
    d = lax.axis_index("dp")
    t = lax.axis_index("tensor")
    z = d // Y
    y = d % Y
    count = [0]
    shared = {}
    drains = []

    class Move:
        def __init__(self, src, dst, device, when=None, key=None):
            i = shared.get(key)
            if i is None:
                i = count[0]
                count[0] += 1
                if key is not None:
                    shared[key] = i
            self.when = when
            self.made = pltpu.make_async_remote_copy(
                src_ref=src,
                dst_ref=dst,
                send_sem=send_sem.at[i],
                recv_sem=recv_sem.at[i],
                device_id=device,
                device_id_type=MESH,
            )

        def start(self):
            self.made.start()
            if self not in drains:
                drains.append(self)

        def wait_recv(self):
            self.made.wait_recv()

        def wait_send(self):
            self.made.wait_send()

    copy = Move

    def at_x(k):
        return (s, d, (t + k) % T)

    def at_y(k):
        return (s, z * Y + (y + k) % Y, t)

    def at_z(k):
        return (s, ((z + k) % Z) * Y + y, t)

    sibling = (1 - s, d, t)

    def far_first(n):
        return sorted(range(1, n), key=lambda k: -min(k, n - k))

    barrier = pltpu.get_barrier_semaphore()
    peers = (
        [at_x(k) for k in range(1, T)]
        + [at_y(k) for k in range(1, Y)]
        + [at_z(k) for k in range(1, Z)]
        + [(1 - s, d, (t + k) % T) for k in range(T)]
    )
    for p in peers:
        pl.semaphore_signal(barrier, inc=1, device_id=p, device_id_type=MESH)

    for c in range(3):
        W["a"][s, z, y, :, c * E : (c + 1) * E] = wq_in[c]
        pack[s, 7:8, c * E : (c + 1) * E] = bq_in[:, c * E : (c + 1) * E]
    W["a"][s, z, y, :, 3 * E :] = wo_in[...]
    W["f"][s, z, y] = wf_in[...]
    W["p"][s, z, y] = wp_in[...]
    pack[s, 0:2, :] = gains_in[...]
    pack[s, 2:6, :] = shifts_in[...]
    pack[s, 6:7, :F] = bf_in[...]
    pl.semaphore_wait(barrier, len(peers))

    pack_copy = copy(pack.at[s], pack.at[s], sibling)
    pack_copy.start()

    def on(core, f):
        pl.when(s == core)(f)

    class Gather:
        def __init__(self, l, m):
            w = W[m]
            self.l = l
            self.direct = (l, m) == (0, "a")
            half = [pl.ds(0, HB), pl.ds(HB, HB)]

            def same(view, device, when, *key):
                return copy(view, view, device, when, ("gather", l, m) + key)

            give = w.at[l, z, y, half[1 - l]]
            self.zero = same(give, sibling, l, 0)
            zs = [(z + k) % Z for k in range(Z)]
            ys = [(y + k) % Y for k in range(Y)]
            self.one, self.two, self.far, self.over = [], [], [], []
            for h in range(2):
                own = w.at[l, z, y, half[h]]
                if h == 0:
                    n, m_, at_one, at_two, ring = Y, Z, at_y, at_z, zs

                    def strip(i, lo=0, size=Y, ring=ring, h=h):
                        return w.at[l, ring[i], pl.ds(lo, size), half[h]]

                else:
                    n, m_, at_one, at_two, ring = Z, Y, at_z, at_y, ys

                    def strip(i, lo=0, size=Z, ring=ring, h=h):
                        return w.at[l, pl.ds(lo, size), ring[i], half[h]]

                self.one.append([same(own, at_one(k), h, 1, k) for k in far_first(n)])
                self.two.append({
                        k: same(strip(0), at_two(k), h, 2, k)
                        for k in (far_first(m_) if self.direct else (1, m_ - 1))
                    })
                self.far.append(
                    {
                        1: same(strip(m_ - 1, 0, n // 2), at_two(1), h, 3, 1),
                        m_ - 1: same(strip(1, n // 2, n // 2), at_two(m_ - 1), h, 3, 2),
                    }
                )
                if h == l:
                    first = [same(strip(0), sibling, h, 4, 0)]
                else:
                    at = [(z, (y + k) % Y) if h == 0 else ((z + k) % Z, y) for k in range(1, n)]
                    first = [
                        same(w.at[l, zz, yy, half[h]], sibling, h, 4, 0, k)
                        for k, (zz, yy) in enumerate(at)
                    ]
                self.over.append([first] + [[same(strip(i), sibling, h, 4, i)] for i in range(1, m_)])

        def s0(self):
            on(self.l, self.zero.start)

        def s1(self, h):
            if h != self.l:
                self.zero.wait_recv()
            for c in self.one[h]:
                c.start()

        def s2(self, h):
            for c in self.one[h]:
                c.wait_recv()
            for c in self.two[h].values():
                c.start()
            for c in self.over[h][0]:
                c.start()

        def s3(self, h):
            for k, c in self.two[h].items():
                if k == 2:
                    continue
                c.wait_recv()
                if not self.direct:
                    self.far[h][k].start()
                self.over[h][1 if k != 1 else len(self.over[h]) - 1][0].start()

        def s4(self, h):
            for c in [self.two[h][2]] if self.direct else self.far[h].values():
                c.wait_recv()
            self.over[h][2][0].start()

        def s5(self, h):
            for group in self.over[1 - h]:
                for c in group:
                    c.wait_recv()

    gathers = [{m: Gather(l, m) for m in names} for l in range(2)]

    def phase(l, *steps):
        for h in range(2):

            def go(h=h):
                for one in steps:
                    getattr(gathers[l][one[0]], one[1:])(h)

            on(h, go)

    def ready(l, m):
        phase(l, m + "s5")

    for l in range(2):
        for m in names:
            gathers[l][m].s0()
    phase(0, "as1", "fs1", "ps1")

    lengths, ranks, micros = (r[...].astype(F32) for r in (len_in, rank_in, micro_in))
    n_seq = lengths.shape[1]
    mine_row = jnp.logical_and(ranks == d.astype(F32), micros == s.astype(F32))
    taken_row = jnp.where(mine_row, lengths, 0.0)
    i0 = lax.broadcasted_iota(jnp.int32, (n_seq, n_seq), 0)
    i1 = lax.broadcasted_iota(jnp.int32, (n_seq, n_seq), 1)
    taken_col = jnp.sum(jnp.where(i0 == i1, taken_row, 0.0), axis=1, keepdims=True)
    ends_col = jnp.sum(jnp.where(i1 <= i0, taken_row, 0.0), axis=1, keepdims=True)
    ends_row = jnp.sum(jnp.where(i0 <= i1, taken_col, 0.0), axis=0, keepdims=True)
    number_row = lax.broadcasted_iota(jnp.int32, (1, n_seq), 1).astype(F32) + 1.0
    number_col = lax.broadcasted_iota(jnp.int32, (n_seq, 1), 0).astype(F32) + 1.0

    def column_labels(rows, first):
        places = (lax.broadcasted_iota(jnp.int32, (rows, n_seq), 0) + first).astype(F32)
        inside = jnp.logical_and(places >= ends_row - taken_row, places < ends_row)
        return jnp.sum(jnp.where(inside, number_row, 0.0), axis=1, keepdims=True)

    label_col = column_labels(R, 0)
    places = lax.broadcasted_iota(jnp.int32, (n_seq, R), 1).astype(F32)
    inside = jnp.logical_and(places >= ends_col - taken_col, places < ends_col)
    label_row = jnp.sum(jnp.where(inside, number_col, 0.0), axis=0, keepdims=True)
    r0 = lax.broadcasted_iota(jnp.int32, (R, R), 0)
    r1 = lax.broadcasted_iota(jnp.int32, (R, R), 1)
    same = jnp.logical_and(label_col == label_row, label_col > 0.5)
    visible = jnp.logical_or(jnp.logical_and(same, r1 <= r0), r0 == r1)
    MASK[...] = jnp.where(visible, 1.0, 0.0)
    valid = [jnp.where(column_labels(HR, t * LR + h * HR) > 0.5, 1.0, 0.0) for h in range(2)]

    pack_copy.wait_recv()

    def gain(l, i):
        return pack[l, i : i + 1, :]

    def shift(l, i):
        return pack[l, 2 + i : 3 + i, :]

    halves = [slice(h * HR, h * HR + HR) for h in range(2)]
    turns = {(h, slot): [] for h in range(2) for slot in range(3)}
    turn = [0, 0]

    def next_turn(h):
        slot = turn[h] % 3
        turn[h] += 1
        for c in turns[h, slot]:
            c.wait_send()
            drains.remove(c)
        return slot

    def gather_x(buf, h):
        slot = next_turn(h)
        part = buf.at[t, pl.ds(h * HR, HR)]
        copies = [copy(part, part, at_x(k), None, ("x", slot, h, k)) for k in far_first(T)]
        for c in copies:
            c.start()
        turns[h, slot] = copies

        def wait():
            for c in copies:
                c.wait_recv()

        return wait

    scatters = [0, 0]

    def scatter_x(part, h):
        slot = next_turn(h)
        number = scatters[h]
        scatters[h] += 1
        turned = number % 2
        stage[turned, h] = part.astype(BF16).reshape(T, HR, D)
        copies = [
            copy(
                stage.at[turned, h, (t + k) % T],
                recv.at[number, h, k - 1],
                at_x(k),
                None,
                ("x", slot, h, k),
            )
            for k in far_first(T)
        ]
        for c in copies:
            c.start()
        turns[h, slot] = copies

        def total():
            for c in copies:
                c.wait_recv()
            v = stage[turned, h, t].astype(F32)
            for k in range(1, T):
                v = v + recv[number, h, k - 1].astype(F32)
            return v

        return total

    lanes = lax.broadcasted_iota(jnp.int32, (R, 2 * HD), 1)

    def half(v, h):
        keep = lanes < HD if h == 0 else lanes >= HD
        return jnp.where(keep, v, jnp.zeros_like(v))

    factor = HD ** (-0.5)

    def some(buf, l, h, lo=None, hi=None):
        v = buf[l, :, halves[h], lo:hi]
        return v.reshape(T * HR, v.shape[-1])

    def every(buf, l, lo=None, hi=None):
        v = buf[l, :, :, lo:hi]
        return v.reshape(R, v.shape[-1])

    def spread(v, n):
        return v.reshape(T, n, v.shape[-1])

    parts_of = {"q": ("a", 0, 3 * E), "o": ("a", 3 * E, 4 * E), "f": ("f", 0, F), "p": ("p", 0, F)}

    def weight(m, l):
        w, lo, hi = parts_of[m]
        return W[w][l, :, :, :, lo:hi].reshape(D, hi - lo)

    def layer_forward(l, inputs_of, at_a, at_q, at_b, at_c, at_d):
        waits = []
        for h in range(2):
            rows = halves[h]
            X = inputs_of[h]()
            n1, inv1 = norm(X)
            N1[l, rows] = n1
            I1[l, rows] = inv1
            HID[rows] = X
            A[l, t, rows] = (n1 * gain(l, 0) + shift(l, 0)).astype(BF16)
            waits.append(gather_x(A.at[l], h))
        at_a()
        ready(l, "a")
        for h in range(2):
            waits[h]()
            v = nn(some(A, l, h), weight("q", l)) + pack[l, 7:8, : 3 * E]
            QKV[l, :, halves[h], :] = spread(v.astype(BF16), HR)
        at_q()
        for pair in range(E // (2 * HD)):
            lo = pair * 2 * HD
            q2, k2, v2 = (every(QKV, l, i * E + lo, i * E + lo + 2 * HD) for i in range(3))
            o2 = None
            for h in range(2):
                S = nt(q2, half(k2, h)) * factor
                S = jnp.where(MASK[...] > 0.5, S, -1e30)
                e = jnp.exp(S - jnp.max(S, axis=-1, keepdims=True))
                pr = (e * (1.0 / jnp.sum(e, axis=-1, keepdims=True))).astype(BF16)
                PR[l, pair * 2 + h] = pr
                part = nn(pr, half(v2, h))
                o2 = part if o2 is None else o2 + part
            O[l, :, :, lo : lo + 2 * HD] = spread(o2.astype(BF16), LR)
        totals = [scatter_x(nt(some(O, l, h), weight("o", l)), h) for h in range(2)]
        at_b()
        waits = []
        for h in range(2):
            rows = halves[h]
            hidden = HID[rows] + totals[h]() + shift(l, 2)
            n2, inv2 = norm(hidden)
            N2[l, rows] = n2
            I2[l, rows] = inv2
            HID[rows] = hidden
            Cn[l, t, rows] = (n2 * gain(l, 1) + shift(l, 1)).astype(BF16)
            waits.append(gather_x(Cn.at[l], h))
        at_c()
        ready(l, "f")
        totals = []
        for h in range(2):
            waits[h]()
            step = F // 2
            for j in range(2):
                cols = slice(j * step, (j + 1) * step)
                u = nn(some(Cn, l, h), W["f"][l, :, :, :, cols].reshape(D, step)) + pack[l, 6:7, cols]
                U[l, :, halves[h], cols] = spread(u, HR)
                Gl[l, :, halves[h], cols] = spread(gelu(u).astype(BF16), HR)
            if h == 0:
                ready(l, "p")
            totals.append(scatter_x(nt(some(Gl, l, h), weight("p", l)), h))
        at_d()
        return [
            lambda h=h: (HID[halves[h]] + totals[h]() + shift(l, 3)) * valid[h] for h in range(2)
        ]

    def grad_matrix(m, l, left, right):
        span = D // Z
        w, lo, hi = parts_of[m]

        def step(i, carry):
            cols = pl.ds(pl.multiple_of(i * span, span), span)
            block = tn(left[:, :, cols].reshape(R, span), right())
            G[w][l, i, :, :, lo:hi] = block.astype(BF16).reshape(Y, B, hi - lo)
            return carry

        lax.fori_loop(0, Z, step, 0)

    class Reduce:
        def __init__(self, l, m):
            self.l, self.m = l, m
            g = G[m]
            half = [pl.ds(0, HB), pl.ds(HB, HB)]
            self.over = [
                copy(g.at[l, :, :, half[1 - h]], SIB[m].at[l], sibling, h, (l, m, 0)) for h in range(2)
            ]
            self.one = [
                [
                    copy(g.at[l, :, (y + k) % Y, half[0]], RA[m].at[l, k - 1], at_y(k), 0, (l, m, 1, k))
                    for k in far_first(Y)
                ],
                [
                    copy(g.at[l, (z + k) % Z, :, half[1]], RA[m].at[l, k - 1], at_z(k), 1, (l, m, 1, k))
                    for k in far_first(Z)
                ],
            ]
            self.two = [
                [
                    copy(g.at[l, (z + k) % Z, y, half[0]], R2[m].at[l, k - 1], at_z(k), 0, (l, m, 2, k))
                    for k in far_first(Z)
                ],
                [
                    copy(g.at[l, z, (y + k) % Y, half[1]], R2[m].at[l, k - 1], at_y(k), 1, (l, m, 2, k))
                    for k in far_first(Y)
                ],
            ]
            self.back = copy(FIN[m].at[0], FIN[m].at[1], sibling, 1 - l)

        def r0(self, h):
            self.over[h].start()

        def r1(self, h):
            g, l, m = G[self.m], self.l, self.m
            rows = slice(h * HB, h * HB + HB)
            self.over[1 - h].wait_recv()

            def step(i, carry):
                g[l, i, :, rows] = (g[l, i, :, rows].astype(F32) + SIB[m][l, i].astype(F32)).astype(BF16)
                return carry

            lax.fori_loop(0, Z, step, 0)
            for c in self.one[h]:
                c.start()

        def r2(self, h):
            g, l, m = G[self.m], self.l, self.m
            rows = slice(h * HB, h * HB + HB)
            for c in self.one[h]:
                c.wait_recv()
            n = len(self.one[h])
            for i in range(n + 1):
                at = (l, i, y, rows) if h == 0 else (l, z, i, rows)
                v = g[at].astype(F32)
                for k in range(n):
                    v = v + RA[m][l, k, i].astype(F32)
                g[at] = v.astype(BF16)
            for c in self.two[h]:
                c.start()

        def r3(self, h):
            g, l, m = G[self.m], self.l, self.m
            rows = slice(h * HB, h * HB + HB)
            for c in self.two[h]:
                c.wait_recv()
            v = g[l, z, y, rows].astype(F32)
            for k in range(len(self.two[h])):
                v = v + R2[m][l, k].astype(F32)
            if h == l:
                put(m, rows, v)
            else:
                FIN[m][0] = v
                self.back.start()

        def r4(self, h):
            if h == self.l:
                self.back.wait_recv()
                put(self.m, slice((1 - h) * HB, (2 - h) * HB), FIN[self.m][1])

    reduces = [{m: Reduce(l, m) for m in names} for l in range(2)]

    def task(l, *steps):
        for h in range(2):

            def go(h=h):
                for one in steps:
                    getattr(reduces[l][one[0]], one[1:])(h)

            on(h, go)

    def hand_over(l, m):
        task(l, m + "r0")

    def column_sum(v):
        return jnp.sum(v, axis=0, keepdims=True)

    def add_small(l, i, h, v):
        v = column_sum(v)
        small[l, i : i + 1, :] = v if h == 0 else small[l, i : i + 1, :] + v

    def layer_backward(l, grads_of, early, at_m, at_c, at_h, at_a):
        waits = []
        for h in range(2):
            dY = grads_of[h]()
            DYS[halves[h]] = dY
            if early is None:
                DM[l, t, halves[h]] = dY.astype(BF16)
                waits.append(gather_x(DM.at[l], h))
            else:
                waits.append(early[h])
            add_small(l, 5, h, dY)
        at_m()
        totals = []
        step = F // 2
        for h in range(2):
            waits[h]()
            for j in range(2):
                cols = slice(j * step, (j + 1) * step)
                dg = nn(some(DM, l, h), W["p"][l, :, :, :, cols].reshape(D, step))
                du = dg * gelu_slope(some(U, l, h, j * step, (j + 1) * step))
                DU[:, halves[h], cols] = spread(du.astype(BF16), HR)
            du = DU[:, halves[h], :].reshape(T * HR, F)
            totals.append(scatter_x(nt(du, weight("f", l)), h))
        grad_matrix("p", l, DM.at[l], lambda: every(Gl, l))
        hand_over(l, "p")
        grad_matrix("f", l, Cn.at[l], lambda: DU[...].reshape(R, F))
        hand_over(l, "f")
        at_c()
        waits = []
        for h in range(2):
            rows = halves[h]
            dc = totals[h]()
            dh = DYS[rows] + norm_back(dc, N2[l, rows], I2[l, rows], gain(l, 1))
            DH[l, t, rows] = dh.astype(BF16)
            waits.append(gather_x(DH.at[l], h))
            HID[rows] = dh
            add_small(l, 1, h, dc * N2[l, rows])
            add_small(l, 3, h, dc)
            add_small(l, 4, h, dh)
        small[l, 6:7, :F] = column_sum(DU[...].reshape(R, F).astype(F32))
        at_h()
        for h in range(2):
            waits[h]()
            DO[:, halves[h], :] = spread(nn(some(DH, l, h), weight("o", l)).astype(BF16), HR)
        if l == 0:
            grad_matrix("o", l, DH.at[l], lambda: every(O, l))
        for pair in range(E // (2 * HD)):
            lo = pair * 2 * HD
            q2, k2, v2 = (every(QKV, l, i * E + lo, i * E + lo + 2 * HD) for i in range(3))
            do2 = DO[:, :, lo : lo + 2 * HD].reshape(R, 2 * HD)
            dq = dk = dv = None
            for h in range(2):
                pr = PR[l, pair * 2 + h]
                p = pr.astype(F32)
                dp = nt(do2, half(v2, h))
                ds = (p * (dp - jnp.sum(p * dp, axis=-1, keepdims=True))).astype(BF16)
                parts = (nn(ds, half(k2, h)), tn(ds, half(q2, h)), tn(pr, half(do2, h)))
                if dq is None:
                    dq, dk, dv = parts
                else:
                    dq, dk, dv = dq + parts[0], dk + parts[1], dv + parts[2]
            for i, v in enumerate((dq * factor, dk * factor, dv)):
                DQKV[:, :, i * E + lo : i * E + lo + 2 * HD] = spread(v.astype(BF16), LR)
        totals = []
        for h in range(2):
            dqkv = DQKV[:, halves[h], :].reshape(T * HR, 3 * E)
            totals.append(scatter_x(nt(dqkv, weight("q", l)), h))
        grad_matrix("q", l, A.at[l], lambda: DQKV[...].reshape(R, 3 * E))
        if l == 1:
            grad_matrix("o", l, DH.at[l], lambda: every(O, l))
        hand_over(l, "a")
        small[l, 7:8, :] = jnp.zeros((1, D), F32)
        small[l, 7:8, : 3 * E] = column_sum(DQKV[...].reshape(R, 3 * E).astype(F32))
        at_a()

        def result(h):
            rows = halves[h]
            da = totals[h]()
            add_small(l, 0, h, da * N1[l, rows])
            add_small(l, 2, h, da)
            return HID[rows] + norm_back(da, N1[l, rows], I1[l, rows], gain(l, 0))

        return [lambda h=h: result(h) for h in range(2)]

    class Small:
        def __init__(self, l):
            self.l = l
            mine = small.at[l]
            self.over = [
                copy(mine, small_sib.at[k], (1 - s, d, (t + k) % T), 1 - l, ("small", 3, k))
                for k in far_first(T) + [0]
            ]
            self.x = [
                copy(mine, small_x.at[k - 1], at_x(k), l, ("small", 0, k)) for k in far_first(T)
            ]
            self.y = [copy(small_x.at[T - 1], small_y.at[k - 1], at_y(k), l, ("small", 1, k)) for k in far_first(Y)]
            self.z = [copy(small_y.at[Y - 1], small_z.at[k - 1], at_z(k), l, ("small", 2, k)) for k in far_first(Z)]

        def begin(self):
            def go(copies):
                for c in copies:
                    c.start()

            on(1 - self.l, lambda: go(self.over))
            on(self.l, lambda: go(self.x))

        def over_x(self):
            for c in self.x + self.over:
                c.wait_recv()
            v = small_x[0] + small_sib[1]
            for k in range(1, T - 1):
                v = v + small_x[k] + small_sib[k + 1]
            row = lax.broadcasted_iota(jnp.int32, v.shape, 0)
            small_x[T - 1] = small[self.l] + small_sib[0] + jnp.where(row < 6, v, 0.0)
            for c in self.y:
                c.start()

        def over_y(self):
            for c in self.y:
                c.wait_recv()
            v = small_x[T - 1]
            for k in range(Y - 1):
                v = v + small_y[k]
            small_y[Y - 1] = v
            for c in self.z:
                c.start()

        def over_z(self):
            for c in self.z:
                c.wait_recv()
            v = small_y[Y - 1]
            for k in range(Z - 1):
                v = v + small_z[k]
            gg_out[...] = v[0:2]
            gs_out[...] = v[2:6]
            gbf_out[...] = v[6:7, :F]
            gbq_out[...] = v[7:8, : 3 * E]

    smalls = [Small(l) for l in range(2)]

    def small_task(l, step):
        on(l, getattr(smalls[l], step))

    act_copy = copy(act_send, act_recv, sibling)
    ig_copy = copy(ig_send, ig_recv, sibling)

    def cot_of(h):
        return cot_in[s, halves[h]].astype(F32) * valid[h]

    early = []

    def gather_cotangent(h):
        part = DM.at[1, t, pl.ds(h * HR, HR)]
        DM[1, t, halves[h]] = cot_of(h).astype(BF16)
        copies = [copy(part, part, at_x(k), None, ("cotangent", h, k)) for k in far_first(T)]
        for c in copies:
            c.start()

        def wait():
            for c in copies:
                c.wait_recv()

        early.append(wait)

    def f0_a():
        for h in range(2):
            gather_cotangent(h)
        phase(0, "as2", "fs2", "as3", "ps2", "as4")

    def f0_q():
        phase(0, "fs3")

    def f0_b():
        phase(0, "ps3", "fs4")
        phase(1, "as1", "fs1", "ps1")

    def f0_c():
        phase(0, "ps4")
        phase(1, "as2", "fs2", "ps2")

    def f0_d():
        phase(1, "as3", "fs3")

    def f1_a():
        phase(1, "ps3", "as4")

    def f1_b():
        phase(1, "fs4", "ps4")

    def nothing():
        pass

    def keep(core, out, send, h, v):
        @pl.when(s == core)
        def _():
            out[core, halves[h]] = v

        @pl.when(s == 1 - core)
        def _():
            send[halves[h]] = v

    def sent(core, move):
        on(1 - core, move.start)

    x_of = [lambda h=h: x_in[s, halves[h]].astype(F32) for h in range(2)]
    y0 = layer_forward(0, x_of, f0_a, f0_q, f0_b, f0_c, f0_d)

    def first_output(h):
        v = y0[h]().astype(BF16)
        keep(0, act_out, act_send, h, v)
        return v.astype(F32)

    y0_of = [lambda h=h: first_output(h) for h in range(2)]

    def f1_start():
        sent(0, act_copy)
        f1_a()

    y1 = layer_forward(1, y0_of, f1_start, nothing, f1_b, nothing, nothing)

    def b1_h():
        task(1, "pr1", "fr1")

    def b1_a():
        task(1, "pr2")

    def b1_c():
        for h in range(2):
            keep(1, act_out, act_send, h, y1[h]().astype(BF16))
        sent(1, act_copy)

    ig1 = layer_backward(1, [lambda h=h: cot_of(h) for h in range(2)], early, nothing, b1_c, b1_h, b1_a)

    def ig1_of(h):
        v = ig1[h]().astype(BF16)
        keep(1, grad_out, ig_send, h, v)
        return v.astype(F32) * valid[h]

    def b0_m():
        sent(1, ig_copy)
        smalls[1].begin()
        task(1, "ar1", "fr2")

    def b0_c():
        task(1, "ar2", "pr3")
        small_task(1, "over_x")

    def b0_h():
        task(0, "pr1", "fr1")
        task(1, "fr3")
        small_task(1, "over_y")

    def b0_a():
        task(0, "ar1", "pr2", "fr2")
        task(1, "ar3")
        small_task(1, "over_z")

    ig0 = layer_backward(0, [lambda h=h: ig1_of(h) for h in range(2)], None, b0_m, b0_c, b0_h, b0_a)
    for h in range(2):
        keep(0, grad_out, ig_send, h, ig0[h]().astype(BF16))
    sent(0, ig_copy)
    smalls[0].begin()

    task(0, "pr3", "fr3")
    small_task(0, "over_x")
    task(0, "ar2")
    small_task(0, "over_y")
    for l, m in ((1, "a"), (1, "f"), (1, "p"), (0, "p"), (0, "f")):
        task(l, m + "r4")
    task(0, "ar3")
    small_task(0, "over_z")
    task(0, "ar4")

    act_copy.wait_recv()
    act_out[1 - s] = act_recv[...]
    ig_copy.wait_recv()
    grad_out[1 - s] = ig_recv[...]

    groups = {}
    for c in drains:
        groups.setdefault(c.when, []).append(c)
    for when, copies in groups.items():

        def drain(copies=copies):
            for c in copies:
                c.wait_send()

        if when is None:
            drain()
        else:
            on(when, drain)
    assert count[0] <= n_sems, count[0]


def split_dp(n):
    root = int(round(n**0.5))
    return n // root, root


def fused(sz, arrays, out_shape):
    names = sz.names
    Z, Y, T, LR, D, E, F, R = sz.Z, sz.Y, sz.T, sz.LR, sz.D, sz.E, sz.F, sz.R
    wd = sz.width
    n_sems = 180
    vm = pltpu.VMEM
    scratch = (
        [vm((2, Z, Y, sz.B, wd[m]), BF16) for m in names]
        + [vm((2, Z, Y, sz.B, wd[m]), BF16) for m in names]
        + [vm((2, Z, Y, sz.HB, wd[m]), BF16) for m in names]
        + [vm((2, Y - 1, Z, sz.HB, wd[m]), BF16) for m in names]
        + [vm((2, Z - 1, sz.HB, wd[m]), BF16) for m in names]
        + [vm((2, sz.HB, wd[m]), F32) for m in names]
        + [vm((2, 8, D), F32)]
        + [vm((2, T, LR, D), BF16)] * 4
        + [
            vm((2, T, LR, 3 * E), BF16),
            vm((2, T, LR, E), BF16),
            vm((2, E // HD, R, R), BF16),
            vm((2, T, LR, F), F32),
            vm((2, T, LR, F), BF16),
        ]
        + [vm((T, LR, F), BF16), vm((T, LR, E), BF16), vm((T, LR, 3 * E), BF16)]
        + [vm((2, LR, D), F32), vm((2, LR, 1), F32), vm((2, LR, D), F32), vm((2, LR, 1), F32)]
        + [vm((LR, D), F32), vm((LR, D), F32), vm((R, R), F32)]
        + [vm((2, 2, T, sz.HR, D), BF16), vm((8, 2, T - 1, sz.HR, D), BF16)]
        + [
            vm((2, 8, D), F32),
            vm((T, 8, D), F32),
            vm((T, 8, D), F32),
            vm((Y, 8, D), F32),
            vm((Z, 8, D), F32),
        ]
        + [vm((LR, D), BF16)] * 4
        + [pltpu.SemaphoreType.DMA((n_sems,)), pltpu.SemaphoreType.DMA((n_sems,))]
    )
    spec = pl.BlockSpec(memory_space=pltpu.VMEM)

    def body(*refs):
        kernel_body(sz, n_sems, *refs)

    return pl.pallas_call(
        body,
        out_shape=out_shape,
        in_specs=[spec] * len(arrays),
        out_specs=[spec] * len(out_shape),
        scratch_shapes=scratch,
        compiler_params=pltpu.CompilerParams(
            collective_id=0, has_side_effects=True, vmem_limit_bytes=62 << 20
        ),
        name="layers",
    )(*arrays)


def hand_out(arrays):
    n = len(arrays)

    def body(*refs):
        sems = refs[2 * n]
        copies = [pltpu.make_async_copy(refs[i], refs[n + i], sems.at[i]) for i in range(n)]
        for c in copies:
            c.start()
        for c in copies:
            c.wait()

    return pl.pallas_call(
        body,
        out_shape=[jax.ShapeDtypeStruct(a.shape, a.dtype) for a in arrays],
        in_specs=[pl.BlockSpec(memory_space=pltpu.VMEM)] * n,
        out_specs=[pl.BlockSpec(memory_space=pl.ANY)] * n,
        scratch_shapes=[pltpu.SemaphoreType.DMA((n,))],
        name="hand_out",
    )(*arrays)


def per_device(*arrays):
    inputs, cotangent, w_qkv, b_qkv, w_out, w_fc, b_fc, w_proj, gains, shifts = arrays[:10]
    Z, Y = split_dp(lax.axis_size("dp"))
    T = lax.axis_size("tensor")
    E = w_qkv.shape[3]
    sz = Sizes(Z, Y, T, inputs.shape[1], inputs.shape[2], E, w_fc.shape[2])
    params = [
        w_qkv[0].transpose(1, 0, 2),
        b_qkv.reshape(1, 3 * E),
        w_out[0].T,
        w_fc[0],
        b_fc,
        w_proj[0].T,
        gains[0],
        shifts[0],
    ]
    seqs = [a.reshape(1, -1) for a in arrays[10:]]
    out_shape = [jax.ShapeDtypeStruct(inputs.shape, BF16)] * 2 + [
        jax.ShapeDtypeStruct(a.shape, F32) for a in params
    ]
    act, grad, gq, gbq, go, gf, gbf, gp, gg, gs = hand_out(
        fused(sz, [inputs, cotangent] + params + seqs, out_shape)
    )
    return (
        act[None],
        grad[None],
        gq.transpose(1, 0, 2)[None],
        gbq.reshape(1, 3, E),
        go.T[None],
        gf[None],
        gbf,
        gp.T[None],
        gg[None],
        gs[None],
    )


def solution(mesh):
    placed = (
        P(None, ("dp", "tensor"), None),
        P(None, ("dp", "tensor"), None),
        P("section", "dp", None, "tensor"),
        P("section", None, "tensor"),
        P("section", "tensor", "dp"),
        P("section", "dp", "tensor"),
        P("section", "tensor"),
        P("section", "tensor", "dp"),
        P("section", None, None),
        P("section", None, None),
        P(),
        P(),
        P(),
    )
    return jax.shard_map(
        per_device,
        mesh=mesh,
        in_specs=placed,
        out_specs=(
            P("section", None, ("dp", "tensor"), None),
            P("section", None, ("dp", "tensor"), None),
            P("section", "dp", None, "tensor"),
            P("section", None, "tensor"),
            P("section", "tensor", "dp"),
            P("section", "dp", "tensor"),
            P("section", "tensor"),
            P("section", "tensor", "dp"),
            P("section", None, None),
            P("section", None, None),
        ),
        check_vma=False,
    )
```
